32 devices in a mesh: group: 2 (over x), expert: 8 (over z, y), tensor: 2 (over core).
Axes of the slice: x: 2, y: 2, z: 4, core: 2. Of those that a mesh axis runs over, the one named last changes fastest.
Arguments:
- residual: bfloat16 [4, 64, 2880], P(None, ('group', 'expert')), parts along dimension 1, may hold values from -6 to 6
- queries: bfloat16 [4, 64, 2048], P(None, ('group', 'expert'), 'tensor'), parts along dimension 1, may hold values from -40 to 40
- new_kv: bfloat16 [4, 64, 2, 256], P(None, ('group', 'expert'), None, 'tensor'), parts along dimension 1, may hold values from -6 to 6
- cache_kv: bfloat16 [64, 256, 2, 256], P(('group', 'expert'), None, None, 'tensor'), parts along dimension 0, may hold values from -40 to 40
- lengths: int32 [64], P(('group', 'expert')), parts along dimension 0, may hold values from 2 to 256, as said below
- routing: int32 [4, 64, 4], P(None, ('group', 'expert')), parts along dimension 1, may hold values from 0 to 7, all different within a row; in each aligned block of 4 rows (0 to 3, 4 to 7, ..., all dimensions but the last counted through in order) at most 4 rows name the same one
- router: bfloat16 [2880, 8], replicated, may hold values from -0.109375 to 0.109375
- out_proj: bfloat16 [2048, 2880], P('tensor'), may hold values from -0.5 to 0.5
- mantissa: bfloat16 [2, 5760, 3, 2880], P('tensor', 'expert'), may hold values from -6 to 6
- exponent: int32 [2, 5760, 3, 90], P('tensor', 'expert'), may hold values from -8 to -6
- placement: int32 [1920], P('group'), parts along dimension 0, may hold values from 0 to 959, as said below
Outputs:
- layer_out: bfloat16 [4, 64, 2880], P(None, ('group', 'expert')), parts along dimension 1
The draws below stay inside these ranges and needn't reach their ends.
There are 2 independent parts, one for each index of `group`. The reference program is written for one: setup_inputs(seed, part) draws one part's arguments, and reference() takes and returns one part's arrays. A program takes and returns all parts, laid end to end along the dimension named above; an argument that names none is the same for every part. Nothing has to cross between parts.
Inputs may be any that keep to these rules, and one draw needn't show every extreme that they name: placement names each learner tile once; learner tile k lies on learner device k // 120; of one owner's slots j * 120 to (j + 1) * 120 - 1 at most 15 take tiles of one learner device, and some take exactly 15. `routing`: each row names 4 different experts; in each aligned block of 4 rows (one device's rows in one step) no expert is named more than 4 times. `lengths`: some row has length 256.
All inputs are finite; a program needn't handle non-finite values.
Results may differ from the reference program's by a relative error of at most 0.0059.
Values may be sent and summed in bfloat16 or wider, within the bound.
No kernel may reach another device: no remote copies, remote signals or barrier semaphores. Data moves between devices by JAX's collectives and lax.ppermute only.
A program may use at most 192 MiB of HBM per device.

```python
import math
import jax
import jax.numpy as jnp
import numpy as np
from jax import lax

D = 2880
FF = 1440
QH = 32
KVH = 4
HD = 64
EXPERTS = 8
TOP = 4
STEPS = 4
BLOCK = 32
TILE_UNITS = 6
ROWS_DEV = 4
LEN = 256
TOKENS = 32
TILES_DEV = 120
TILES = 960
MOST = 15
CAP = 4
N_EXPERT = 8
N_TENSOR = 2


def draw_queries(key, part):
    key = jax.random.fold_in(key, 1)
    values_drawn = jnp.clip(jax.random.normal(key, (STEPS, TOKENS, KVH, QH // KVH, HD), jnp.float32), -4.0, 4.0)
    return values_drawn.reshape(STEPS, TOKENS, QH * HD).astype(jnp.bfloat16)


def draw_cache_kv(key, part):
    key = jax.random.fold_in(key, 2)
    values_drawn = jnp.clip(jax.random.normal(key, (TOKENS, LEN, 2, KVH, HD), jnp.float32), -4.0, 4.0)
    return values_drawn.reshape(TOKENS, LEN, 2, KVH * HD).astype(jnp.bfloat16)


def draw_lengths(key, part):
    key = jax.random.fold_in(key, 3)
    first_key, second_key = jax.random.split(key)
    lengths_drawn = jax.random.randint(first_key, (TOKENS,), 2, LEN + 1, dtype=jnp.int32)
    longest = jax.random.randint(second_key, (), 0, TOKENS, dtype=jnp.int32)
    return lengths_drawn.at[longest].set(LEN).astype(jnp.int32)


def draw_placement(key, part):
    key = jax.random.fold_in(key, 4)
    relabel_key, owner_key, offset_key = jax.random.split(key, 3)
    relabel_src = jax.random.permutation(relabel_key, N_EXPERT)
    relabel_dst = jax.random.permutation(owner_key, N_EXPERT)
    offsets = jax.random.permutation(offset_key, N_EXPERT)
    positions = jnp.arange(TILES_DEV, dtype=jnp.int32)
    shift_pos = offsets[positions // MOST]
    source_dev = relabel_src[(relabel_dst[:, None] + shift_pos[None, :]) % N_EXPERT]
    return (source_dev * TILES_DEV + positions[None, :]).reshape(TILES).astype(jnp.int32)


def touch_ends(entries, stream_key, smallest, largest):
    index_at = [jax.random.randint(jax.random.fold_in(stream_key, axis), (), 0, length) for axis, length in enumerate(entries.shape)]
    widest = entries.shape.index(max(entries.shape))
    beside = index_at[:widest] + [(index_at[widest] + 1) % entries.shape[widest]] + index_at[widest + 1:]
    return entries.at[tuple(index_at)].set(smallest).at[tuple(beside)].set(largest)


def level_of(key, shape, pieces, low, largest):
    gain, own = 1.0, jax.random.fold_in(key, 6)
    for axis_at, blocks in pieces:
        heights = jnp.exp(jax.random.uniform(jax.random.fold_in(own, axis_at), (blocks,), jnp.float32, low / len(pieces), largest / len(pieces)))
        gain = gain * jnp.repeat(heights, shape[axis_at] // blocks).reshape([-1 if axis == axis_at else 1 for axis in range(len(shape))])
    return gain


def deal_out(rng, own, number, rows, count, top, limit, slope):
    order = jax.random.permutation(rng, count)
    heavy_load, common = shares(count, rows * top, limit, slope, True), shares(count, rows * top, limit, slope, False)
    places = jnp.arange(count)

    def named(tallies, turn):
        used = int((tallies > 0).sum())
        fixed = max(1, used // 4)
        moved = fixed + (places - fixed + turn * (used - fixed)) % max(1, count - fixed)
        return jnp.zeros((count,), jnp.int32).at[order[jnp.where(places < fixed, places, moved)]].set(jnp.asarray(tallies, jnp.int32))

    tallies = jnp.where(number % 4 == 0, named(heavy_load, number // 4), named(common, number - number // 4 - 1))
    mixed = jax.random.permutation(jax.random.fold_in(own, 3), count)
    giver, taker = mixed[0:count // 2 * 2:2], mixed[1:count // 2 * 2:2]
    slack = jnp.minimum(tallies[giver] - 1, limit - tallies[taker]) // 2
    slack = jnp.where((giver == order[0]) | (taker == order[0]) | (tallies[taker] == 0), 0, jnp.maximum(slack, 0))
    moved = jax.random.randint(jax.random.fold_in(own, 4), (count // 2,), 0, 1 << 20) % (slack + 1)
    tallies = tallies.at[giver].add(-moved).at[taker].add(moved)
    members = jnp.searchsorted(jnp.cumsum(tallies), jnp.arange(rows * top), side="right").astype(jnp.int32)
    table = members.reshape(top, rows).T
    table = table[jax.random.permutation(jax.random.fold_in(own, 1), rows)]
    turn = jax.random.randint(jax.random.fold_in(own, 2), (rows, 1), 0, top)
    return jnp.take_along_axis(table, (jnp.arange(top)[None, :] + turn) % top, axis=1)


def shares(amount, total, bound, lean, full):
    portions = [(1 << 20) // math.isqrt(standing ** lean) + 1 for standing in range(1, amount + 1)]
    largest = bound if full else min(bound, max(-(-total // amount), total * portions[0] // sum(portions)))
    least = 1 if total - largest >= amount - 1 else 0
    holding, spare = [largest] + [least] * (amount - 1), total - largest - least * (amount - 1)
    while spare > 0:
        movable = [i for i in range(1, amount) if holding[i] < largest] or [i for i in range(1, amount) if holding[i] < bound]
        mass, budget = sum([portions[i] for i in movable]), spare
        for i in movable:
            extra = min(bound - holding[i], max(1, budget * portions[i] // mass), spare)
            holding[i] = holding[i] + extra
            spare = spare - extra
    return np.array(holding)


def centred(stream_key, extent, spread, bound, shards=(), kind=jnp.bfloat16):
    result = spread * jax.random.normal(stream_key, extent, jnp.float32)
    if shards:
        result = result * level_of(stream_key, extent, shards, -0.22, 0.18)
    return jnp.clip(result, -bound, bound).astype(kind)


def setup_inputs(seed: int = 0, part: int = 0) -> dict:
    streams_of = jax.random.split(jax.random.key(seed), 12)
    part_keys = jax.random.split(jax.random.fold_in(streams_of[11], part), 12)
    residual = centred(part_keys[0], (STEPS, TOKENS, D), 1.0, 6.0, ((1, 8),))
    queries = draw_queries(jax.random.fold_in(jax.random.fold_in(streams_of[11], part), 71), part)
    new_kv = centred(part_keys[2], (STEPS, TOKENS, 2, KVH * HD), 1.0, 6.0, ((1, 8), (3, 2)))
    cache_kv = draw_cache_kv(jax.random.fold_in(jax.random.fold_in(streams_of[11], part), 71), part)
    lengths = draw_lengths(jax.random.fold_in(jax.random.fold_in(streams_of[11], part), 71), part)
    routing_keys = jax.random.split(jax.random.fold_in(part_keys[5], 1), STEPS * TOKENS // ROWS_DEV)
    routing_turns = jax.random.permutation(jax.random.fold_in(part_keys[5], 3), STEPS * TOKENS // ROWS_DEV)
    routing = jax.vmap(lambda own, number: deal_out(jax.random.fold_in(part_keys[5], 2), own, number, ROWS_DEV, EXPERTS, TOP, CAP, 2))(routing_keys, routing_turns).reshape((STEPS, TOKENS, TOP))
    router = centred(streams_of[6], (D, EXPERTS), D ** -0.5, 0.109375)
    out_proj = centred(streams_of[7], (QH * HD, D), (QH * HD // 16) ** -0.5, 0.5, ((0, 2),))
    mantissa = jnp.clip(jax.random.uniform(streams_of[8], (N_TENSOR, TILES * TILE_UNITS, 3, D), jnp.float32, -6.0, 6.0) * level_of(streams_of[8], (N_TENSOR, TILES * TILE_UNITS, 3, D), ((0, 2), (1, 8)), -0.4, 0.0), -6.0, 6.0).astype(jnp.bfloat16)
    exponent = touch_ends(jax.random.randint(streams_of[9], (N_TENSOR, TILES * TILE_UNITS, 3, D // BLOCK), -3 - 5 * D // 2880, 0 - 5 * D // 2880), jax.random.fold_in(streams_of[9], 1), -3 - 5 * D // 2880, (0 - 5 * D // 2880) - 1).astype(jnp.int32)
    placement = draw_placement(jax.random.fold_in(jax.random.fold_in(streams_of[11], part), 71), part)
    return {"residual": residual, "queries": queries, "new_kv": new_kv, "cache_kv": cache_kv, "lengths": lengths, "routing": routing, "router": router, "out_proj": out_proj, "mantissa": mantissa, "exponent": exponent, "placement": placement}


def dequantize(mantissa, exponent):
    full_shape = mantissa.shape
    scale_power = jnp.exp2(exponent.astype(jnp.float32))
    blocks = mantissa.astype(jnp.float32).reshape(full_shape[:-1] + (full_shape[-1] // BLOCK, BLOCK))
    return (blocks * scale_power[..., None]).reshape(full_shape).astype(jnp.bfloat16)

def reference(residual, queries, new_kv, cache_kv, lengths, routing, router, out_proj, mantissa, exponent, placement):
    weights = dequantize(mantissa, exponent)
    tiled = weights.reshape(N_TENSOR, TILES, TILE_UNITS, 3, D)[:, placement]
    experts = tiled.reshape(N_TENSOR, EXPERTS, FF // N_TENSOR, 3, D).transpose(1, 0, 2, 3, 4).reshape(EXPERTS, FF, 3, D)
    query_group = QH // KVH
    scale_factor = 1.0 / math.sqrt(HD)
    cache_keys = cache_kv[:, :, 0].astype(jnp.float32).reshape(TOKENS, LEN, KVH, HD)
    cache_values = cache_kv[:, :, 1].astype(jnp.float32).reshape(TOKENS, LEN, KVH, HD)
    alive = jnp.arange(LEN)[None, :] < lengths[:, None]
    collected = []
    for step_index in range(STEPS):
        queries_now = queries[step_index].astype(jnp.float32).reshape(TOKENS, KVH, query_group, HD)
        fresh_kv = new_kv[:step_index + 1].astype(jnp.float32).reshape(step_index + 1, TOKENS, 2, KVH, HD)
        all_keys = jnp.concatenate([cache_keys, fresh_kv[:, :, 0].transpose(1, 0, 2, 3)], axis=1)
        all_values = jnp.concatenate([cache_values, fresh_kv[:, :, 1].transpose(1, 0, 2, 3)], axis=1)
        allowed = jnp.concatenate([alive, jnp.ones((TOKENS, step_index + 1), dtype=bool)], axis=1)
        scores = jnp.einsum('tgqd,tlgd->tgql', queries_now, all_keys) * scale_factor
        scores = jnp.where(allowed[:, None, None, :], scores, -1e+30)
        highest = lax.optimization_barrier(jnp.max(scores, axis=-1, keepdims=True))
        raised = jnp.exp(scores - highest)
        probability = (raised / lax.optimization_barrier(jnp.sum(raised, axis=-1, keepdims=True))).astype(jnp.bfloat16)
        heads_out = jnp.einsum('tgql,tlgd->tgqd', probability.astype(jnp.float32), all_values)
        heads_out = heads_out.astype(jnp.bfloat16).reshape(TOKENS, QH * HD)
        mixed = residual[step_index].astype(jnp.float32) + jnp.dot(heads_out, out_proj, preferred_element_type=jnp.float32)
        normed = (mixed * lax.rsqrt(lax.optimization_barrier(jnp.mean(mixed * mixed, axis=-1, keepdims=True)) + 1e-05)).astype(jnp.bfloat16)
        logits = jnp.dot(normed, router, preferred_element_type=jnp.float32)
        chosen = jnp.take_along_axis(logits, routing[step_index], axis=1)
        sigmoids = jax.nn.sigmoid(chosen)
        gate_values = sigmoids / lax.optimization_barrier(jnp.sum(sigmoids, axis=-1, keepdims=True))

        def expert_out(matrix):
            gate_part = jnp.dot(normed, matrix[:, 0, :].T, preferred_element_type=jnp.float32)
            up_part = jnp.dot(normed, matrix[:, 1, :].T, preferred_element_type=jnp.float32)
            hidden = (jax.nn.silu(gate_part) * up_part).astype(jnp.bfloat16)
            return jnp.dot(hidden, matrix[:, 2, :], preferred_element_type=jnp.float32)
        results = lax.map(expert_out, experts)
        picked = results[routing[step_index], jnp.arange(TOKENS)[:, None]]
        moe_sum = lax.optimization_barrier(jnp.sum(picked * gate_values[:, :, None], axis=1))
        collected.append((mixed + moe_sum).astype(jnp.bfloat16))
    return jnp.stack(collected)
```

```python
import functools

import jax
import jax.numpy as jnp
from jax import lax
from jax.experimental import pallas as pl
from jax.experimental.pallas import tpu as pltpu
from jax.sharding import PartitionSpec as P

HD = 64
EXPERTS = 8
TOP = 4
BLOCK = 32
TILE_UNITS = 6
LANES = 128
F32 = jnp.float32
BF16 = jnp.bfloat16
VMEM_LIMIT = 56 * 1024 * 1024

NT = (((1,), (1,)), ((), ()))
TN = (((0,), (0,)), ((), ()))


def dot(a, b, dims=(((1,), (0,)), ((), ()))):
    return lax.dot_general(a, b, dims, preferred_element_type=F32)


def iota(shape, dim):
    return lax.broadcasted_iota(jnp.int32, shape, dim)


def attention_kernel(
    steps, rows, lengths_ref, queries_ref, fresh_ref, cache_ref, proj_hbm, out_ref, packed, mixed, proj, sem
):
    copy = pltpu.make_async_copy(proj_hbm, proj, sem)
    copy.start()
    count = steps * rows
    groups = queries_ref.shape[1] // LANES
    half = groups // 2
    lane = iota((count, LANES), 1)
    for group in range(groups):
        piece = queries_ref[:, group * LANES : (group + 1) * LANES].astype(F32) * (HD**-0.5)
        mine = (lane < HD) == (group < half)
        packed[group * count : (group + 1) * count, :] = jnp.where(mine, piece, 0.0)
        packed[(groups + group) * count : (groups + group + 1) * count, :] = jnp.where(
            mine, pltpu.roll(piece, HD, 1), 0.0
        )
    amount = 2 * groups * steps
    span = cache_ref.shape[1]
    fresh = fresh_ref[...]
    width = fresh.shape[0]
    spot = iota((amount, span), 1)
    step_of = iota((amount, width), 0) % steps
    fresh_spot = iota((amount, width), 1)
    fresh_step = fresh_spot // (2 * rows)
    for row in range(rows):
        now = packed[pl.ds(row, amount, stride=rows), :].astype(BF16)
        cache = cache_ref[row]
        scores = dot(now, cache, NT)
        live = (spot % 2 == 0) & (spot < 2 * lengths_ref[row])
        scores = jnp.where(live, scores, -1e30)
        late = dot(now, fresh, NT)
        seen = (fresh_spot % (2 * rows) == 2 * row) & (fresh_step <= step_of)
        late = jnp.where(seen, late, -1e30)
        highest = jnp.maximum(
            jnp.max(scores, axis=1, keepdims=True), jnp.max(late, axis=1, keepdims=True)
        )
        scores = jnp.exp(scores - highest)
        late = jnp.exp(late - highest)
        total = jnp.sum(scores, axis=1, keepdims=True) + jnp.sum(late, axis=1, keepdims=True)
        probs = pltpu.roll(scores / total, 1, 1).astype(BF16)
        late_probs = pltpu.roll(late / total, 1, 1).astype(BF16)
        mixed[pl.ds(row, amount, stride=rows), :] = dot(probs, cache) + dot(late_probs, fresh)
    heads = []
    for group in range(groups):
        straight = mixed[group * count : (group + 1) * count, :]
        turned = mixed[(groups + group) * count : (groups + group + 1) * count, :]
        mine = (lane < HD) == (group < half)
        heads.append(jnp.where(mine, straight, pltpu.roll(turned, HD, 1)).astype(BF16))
    copy.wait()
    out_ref[...] = dot(jnp.concatenate(heads, axis=1), proj[...], NT)


def attend(lengths, queries, new_kv, cache_kv, out_proj):
    steps, rows, width = queries.shape
    span = cache_kv.shape[1]
    proj = out_proj.T
    model_width = proj.shape[0]
    count = steps * rows
    groups = width // LANES
    fresh = new_kv.reshape(steps * rows * 2, LANES)
    fresh = jnp.pad(fresh, ((0, -fresh.shape[0] % LANES), (0, 0)))
    return pl.pallas_call(
        functools.partial(attention_kernel, steps, rows),
        out_shape=jax.ShapeDtypeStruct((count, model_width), F32),
        in_specs=[
            pl.BlockSpec(memory_space=pltpu.SMEM),
            pl.BlockSpec(memory_space=pltpu.VMEM),
            pl.BlockSpec(memory_space=pltpu.VMEM),
            pl.BlockSpec(memory_space=pltpu.VMEM),
            pl.BlockSpec(memory_space=pl.ANY),
        ],
        out_specs=pl.BlockSpec(memory_space=pltpu.VMEM),
        scratch_shapes=[
            pltpu.VMEM((2 * groups * count, LANES), F32),
            pltpu.VMEM((2 * groups * count, LANES), F32),
            pltpu.VMEM(proj.shape, BF16),
            pltpu.SemaphoreType.DMA,
        ],
        compiler_params=pltpu.CompilerParams(vmem_limit_bytes=VMEM_LIMIT),
        cost_estimate=pl.CostEstimate(flops=2 * count * width * model_width, bytes_accessed=7 << 20, transcendentals=0),
        name="attention",
    )(lengths, queries.reshape(count, width), fresh, cache_kv.reshape(rows, 2 * span, LANES), proj)


def norm_kernel(residual_ref, mine_ref, other_ref, routing_ref, router_ref, mixed_ref, packed_ref):
    width = residual_ref.shape[1]
    mixed = residual_ref[...].astype(F32) + (mine_ref[...] + other_ref[...])
    mixed_ref[...] = mixed
    scale = lax.rsqrt(jnp.mean(mixed * mixed, axis=1, keepdims=True) + 1e-05)
    normed = (mixed * scale).astype(BF16)
    logits = dot(normed, router_ref[...], NT)
    routing = routing_ref[...]
    expert = iota(logits.shape, 1)
    chosen = expert == routing[:, 0:1]
    for slot in range(1, TOP):
        chosen = chosen | (expert == routing[:, slot : slot + 1])
    sigmoids = jnp.where(chosen, jax.nn.sigmoid(logits), 0.0)
    gates = sigmoids / jnp.sum(sigmoids, axis=1, keepdims=True)
    high = gates.astype(BF16)
    low = (gates - high.astype(F32)).astype(BF16)
    first = width // LANES * LANES
    offset = width - first
    target = iota((EXPERTS, LANES), 1) - iota((EXPERTS, LANES), 0)
    tail = dot(high, (target == offset).astype(BF16)) + dot(low, (target == offset + EXPERTS).astype(BF16))
    packed_ref[:, :width] = normed
    packed_ref[:, width : width + LANES - offset] = tail[:, offset:].astype(BF16)


def normalize(residual, mine, other, routing, router):
    count, width = residual.shape
    padded = -(-(width + 2 * EXPERTS) // LANES) * LANES
    return pl.pallas_call(
        norm_kernel,
        out_shape=(
            jax.ShapeDtypeStruct((count, width), F32),
            jax.ShapeDtypeStruct((count, padded), BF16),
        ),
        compiler_params=pltpu.CompilerParams(vmem_limit_bytes=VMEM_LIMIT),
        name="normalize",
    )(residual, mine, other, routing, router.T)


def weights_kernel(mantissa_ref, exponent_ref, out_ref):
    blocks, units = exponent_ref.shape[1], exponent_ref.shape[2]
    width = mantissa_ref.shape[2]
    expander = (iota((blocks, width), 1) // BLOCK == iota((blocks, width), 0)).astype(BF16)
    power = jnp.exp2(exponent_ref[0].astype(F32)).astype(BF16)
    scale = dot(power, expander, TN)
    out_ref[0] = (mantissa_ref[0].astype(F32) * scale).astype(BF16)


def dequantize(mantissa, exponent):
    units, parts, width = mantissa.shape
    blocks = exponent.shape[2]
    step = units
    mantissa = mantissa.transpose(1, 0, 2)
    exponent = exponent.transpose(1, 2, 0)
    return pl.pallas_call(
        weights_kernel,
        grid=(parts,),
        out_shape=jax.ShapeDtypeStruct((parts, units, width), BF16),
        in_specs=[
            pl.BlockSpec((1, step, width), lambda part: (part, 0, 0)),
            pl.BlockSpec((1, blocks, step), lambda part: (part, 0, 0)),
        ],
        out_specs=pl.BlockSpec((1, step, width), lambda part: (part, 0, 0)),
        compiler_params=pltpu.CompilerParams(vmem_limit_bytes=VMEM_LIMIT),
        cost_estimate=pl.CostEstimate(flops=2 * parts * units * blocks * width, bytes_accessed=4 * parts * units * width, transcendentals=0),
        name="weights",
    )(mantissa, exponent)


def experts_kernel(count, width, gate_ref, up_ref, down_ref, member_ref, *refs):
    arrived, (mine_ref, other_ref, rows, gates, total) = refs[:-5], refs[-5:]
    step = pl.program_id(0)

    @pl.when(step == 0)
    def _():
        place = 0
        for ref in arrived:
            rows[place : place + ref.shape[0], :] = ref[...]
            place += ref.shape[0]
        total[...] = jnp.zeros_like(total)
        gates[...] = rows[:, width : width + 2 * EXPERTS]

    inputs = rows[:, :width]
    gate = dot(inputs, gate_ref[0], NT)
    up = dot(inputs, up_ref[0], NT)
    member = member_ref[0]
    share = dot(gates[:, :EXPERTS], member) + dot(gates[:, EXPERTS:], member)
    hidden = (gate * jax.nn.sigmoid(gate) * up * share).astype(BF16)
    total[...] += dot(hidden, down_ref[0])

    @pl.when(step == pl.num_programs(0) - 1)
    def _():
        half = total.shape[0] // 2
        mine_ref[...] = total[:half, :]
        other_ref[...] = total[half:, :].astype(BF16)


def unit_step(units):
    for step in range(240, 15, -16):
        if units % step == 0:
            return step
    return units


def run_experts(weights, member, arrived):
    parts, units, width = weights.shape
    count = sum(block.shape[0] for block in arrived)
    padded = arrived[0].shape[1]
    step = unit_step(units)
    member = member.reshape(EXPERTS, units // step, step).transpose(1, 0, 2)
    part = lambda which: pl.BlockSpec((1, step, width), lambda place: (which, place, 0))
    whole = lambda shape: pl.BlockSpec(shape, lambda place: (0, 0))
    return pl.pallas_call(
        functools.partial(experts_kernel, count, width),
        grid=(units // step,),
        out_shape=(
            jax.ShapeDtypeStruct((count // 2, width), F32),
            jax.ShapeDtypeStruct((count // 2, width), BF16),
        ),
        in_specs=[part(0), part(1), part(2), pl.BlockSpec((1, EXPERTS, step), lambda place: (place, 0, 0))]
        + [whole(block.shape) for block in arrived],
        out_specs=(whole((count // 2, width)), whole((count // 2, width))),
        scratch_shapes=[
            pltpu.VMEM((count, padded), BF16),
            pltpu.VMEM((count, 2 * EXPERTS), BF16),
            pltpu.VMEM((count, width), F32),
        ],
        compiler_params=pltpu.CompilerParams(vmem_limit_bytes=VMEM_LIMIT),
        cost_estimate=pl.CostEstimate(flops=6 * count * units * width, bytes_accessed=6 * units * width, transcendentals=0),
        name="experts",
    )(weights, weights, weights, member, *arrived)


def swap(value):
    return lax.ppermute(value, "tensor", [(0, 1), (1, 0)])


def partners(count):
    half = count // 2
    power = count & (count - 1) == 0
    reach = lambda place, far: place ^ far if power else (place + far) % count
    turns = []
    for turn in range(half):
        pairs = []
        for place in range(count):
            pairs.append((2 * place, 2 * reach(place, turn)))
            pairs.append((2 * place + 1, 2 * reach(place, turn + half) + 1))
        turns.append(pairs)
    return turns


def per_device(residual, queries, new_kv, cache_kv, lengths, routing, router, out_proj, mantissa, exponent, placement):
    places = lax.axis_size("expert")
    place = lax.axis_index("expert")
    steps, rows, width = residual.shape
    count = steps * rows
    units = mantissa.shape[1]
    turns = partners(places)
    both = ("expert", "tensor")

    partial = attend(lengths, queries, new_kv, cache_kv, out_proj)
    weights = dequantize(mantissa[0], exponent[0])
    tile = place * (units // TILE_UNITS) + jnp.arange(units) // TILE_UNITS
    member = jnp.any(placement.reshape(EXPERTS, -1, 1) == tile, axis=1).astype(BF16)

    mixed, packed = normalize(
        residual.reshape(count, width), partial, swap(partial), routing.reshape(count, TOP), router
    )
    near = [lax.ppermute(packed, both, pairs) for pairs in turns]
    far = [swap(block) for block in near]
    mine, other = run_experts(weights, member, near + far)
    mine = mine + swap(other).astype(F32)
    back = [
        lax.ppermute(mine[turn * count : (turn + 1) * count].astype(BF16), both, [(to, back) for back, to in pairs])
        for turn, pairs in enumerate(turns)
    ]
    total = sum(block.astype(F32) for block in back)
    result = mixed + (total + swap(total))
    return result.astype(BF16).reshape(steps, rows, width)


def solution(mesh):
    placed = (
        P(None, ("group", "expert"), None),
        P(None, ("group", "expert"), "tensor"),
        P(None, ("group", "expert"), None, "tensor"),
        P(("group", "expert"), None, None, "tensor"),
        P(("group", "expert")),
        P(None, ("group", "expert"), None),
        P(),
        P("tensor", None),
        P("tensor", "expert", None, None),
        P("tensor", "expert", None, None),
        P("group"),
    )
    return jax.shard_map(
        per_device,
        mesh=mesh,
        in_specs=placed,
        out_specs=P(None, ("group", "expert"), None),
        check_vma=False,
    )
```

```python
import functools

import jax
import jax.numpy as jnp
from jax import lax
from jax.experimental import pallas as pl
from jax.experimental.pallas import tpu as pltpu
from jax.sharding import PartitionSpec as P

HD = 64
EXPERTS = 8
TOP = 4
BLOCK = 32
TILE_UNITS = 6
LANES = 128
AHEAD = 3
F32 = jnp.float32
BF16 = jnp.bfloat16

NT = (((1,), (1,)), ((), ()))
TN = (((0,), (0,)), ((), ()))
TT = (((0,), (1,)), ((), ()))


def dot(a, b, dims=(((1,), (0,)), ((), ()))):
    return lax.dot_general(a, b, dims, preferred_element_type=F32)


def iota(shape, dim):
    return lax.broadcasted_iota(jnp.int32, shape, dim)


def vmem(shape, dtype):
    return pltpu.VMEM(shape, dtype)


def held(value):
    return pltpu.with_memory_space_constraint(value, pltpu.VMEM)


def afar(value):
    return pltpu.with_memory_space_constraint(value, pltpu.HBM)


def whole(count):
    return [pl.BlockSpec(memory_space=pltpu.VMEM)] * count


def params(mebibytes=8):
    return pltpu.CompilerParams(vmem_limit_bytes=mebibytes << 20)


def attention_kernel(
    lengths_ref,
    queries_hbm,
    fresh_hbm,
    cache_hbm,
    proj_hbm,
    out_ref,
    queries,
    fresh_rows,
    cache_rows,
    proj,
    packed,
    mixed,
    sems,
):
    late_width = fresh_hbm.shape[0]
    fresh_rows[...] = jnp.zeros_like(fresh_rows)
    moves = [
        pltpu.make_async_copy(queries_hbm, queries, sems.at[0]),
        pltpu.make_async_copy(fresh_hbm, fresh_rows.at[:late_width], sems.at[1]),
        pltpu.make_async_copy(cache_hbm, cache_rows, sems.at[2]),
        pltpu.make_async_copy(proj_hbm, proj, sems.at[3]),
    ]
    for move in moves:
        move.start()
    steps, rows, _ = queries.shape
    count = steps * rows
    groups = queries.shape[2] // LANES
    half = groups // 2
    lane = iota((rows, LANES), 1)
    moves[0].wait()
    for step in range(steps):
        for group in range(groups):
            piece = queries[step, :, group * LANES : (group + 1) * LANES].astype(F32) * (HD**-0.5)
            mine = (lane < HD) == (group < half)
            first = group * count + step * rows
            packed[first : first + rows, :] = jnp.where(mine, piece, 0.0)
            first += groups * count
            packed[first : first + rows, :] = jnp.where(mine, pltpu.roll(piece, HD, 1), 0.0)
    amount = 2 * groups * steps
    span = cache_rows.shape[1]
    width = fresh_rows.shape[0]
    spot = iota((amount, span), 1)
    step_of = iota((amount, width), 0) % steps
    fresh_spot = iota((amount, width), 1)
    fresh_step = fresh_spot // (2 * rows)
    moves[1].wait()
    moves[2].wait()
    fresh = fresh_rows[...]
    for row in range(rows):
        now = packed[pl.ds(row, amount, stride=rows), :].astype(BF16)
        cache = cache_rows[row]
        scores = dot(now, cache, NT)
        live = (spot % 2 == 0) & (spot < 2 * lengths_ref[row])
        scores = jnp.where(live, scores, -1e30)
        late = dot(now, fresh, NT)
        seen = (fresh_spot % (2 * rows) == 2 * row) & (fresh_step <= step_of)
        late = jnp.where(seen, late, -1e30)
        highest = jnp.maximum(
            jnp.max(scores, axis=1, keepdims=True), jnp.max(late, axis=1, keepdims=True)
        )
        scores = jnp.exp(scores - highest)
        late = jnp.exp(late - highest)
        total = jnp.sum(scores, axis=1, keepdims=True) + jnp.sum(late, axis=1, keepdims=True)
        probs = pltpu.roll(scores / total, 1, 1).astype(BF16)
        late_probs = pltpu.roll(late / total, 1, 1).astype(BF16)
        mixed[pl.ds(row, amount, stride=rows), :] = dot(probs, cache) + dot(late_probs, fresh)
    heads = []
    lane = iota((count, LANES), 1)
    for group in range(groups):
        straight = mixed[group * count : (group + 1) * count, :]
        turned = mixed[(groups + group) * count : (groups + group + 1) * count, :]
        mine = (lane < HD) == (group < half)
        heads.append(jnp.where(mine, straight, pltpu.roll(turned, HD, 1)).astype(BF16))
    moves[3].wait()
    out_ref[...] = dot(jnp.concatenate(heads, axis=1), proj[...], NT)


def attend(lengths, queries, new_kv, cache_kv, out_proj):
    steps, rows, width = queries.shape
    span = cache_kv.shape[1]
    proj = out_proj.T
    model_width = proj.shape[0]
    count = steps * rows
    groups = width // LANES
    fresh = new_kv.reshape(count * 2, LANES)
    cache = cache_kv.reshape(rows, 2 * span, LANES)
    padded = -(-fresh.shape[0] // LANES) * LANES
    return pl.pallas_call(
        attention_kernel,
        out_shape=vmem((count, model_width), F32),
        in_specs=[pl.BlockSpec(memory_space=pltpu.SMEM)] + [pl.BlockSpec(memory_space=pltpu.HBM)] * 4,
        out_specs=pl.BlockSpec(memory_space=pltpu.VMEM),
        scratch_shapes=[
            pltpu.VMEM(queries.shape, BF16),
            pltpu.VMEM((padded, LANES), BF16),
            pltpu.VMEM(cache.shape, BF16),
            pltpu.VMEM(proj.shape, BF16),
            pltpu.VMEM((2 * groups * count, LANES), F32),
            pltpu.VMEM((2 * groups * count, LANES), F32),
            pltpu.SemaphoreType.DMA((4,)),
        ],
        compiler_params=params(16),
        cost_estimate=pl.CostEstimate(
            flops=2 * count * width * model_width, bytes_accessed=7 << 20, transcendentals=0
        ),
        name="attention",
    )(lengths, afar(queries), afar(fresh), afar(cache), afar(proj))


def norm_kernel(residual_ref, mine_ref, other_ref, routing_ref, router_ref, mixed_ref, packed_ref):
    steps, rows, width = residual_ref.shape
    for step in range(steps):
        mixed_ref[step * rows : (step + 1) * rows, :] = residual_ref[step].astype(F32)
    mixed = mixed_ref[...] + (mine_ref[...] + other_ref[...])
    mixed_ref[...] = mixed
    scale = lax.rsqrt(jnp.mean(mixed * mixed, axis=1, keepdims=True) + 1e-05)
    normed = (mixed * scale).astype(BF16)
    logits = dot(normed, router_ref[...], NT)
    routing = routing_ref[...]
    expert = iota(logits.shape, 1)
    chosen = expert == routing[:, 0:1]
    for slot in range(1, TOP):
        chosen = chosen | (expert == routing[:, slot : slot + 1])
    sigmoids = jnp.where(chosen, jax.nn.sigmoid(logits), 0.0)
    gates = sigmoids / jnp.sum(sigmoids, axis=1, keepdims=True)
    high = gates.astype(BF16)
    low = (gates - high.astype(F32)).astype(BF16)
    first = width // LANES * LANES
    offset = width - first
    target = iota((EXPERTS, LANES), 1) - iota((EXPERTS, LANES), 0)
    tail = dot(high, (target == offset).astype(BF16)) + dot(low, (target == offset + EXPERTS).astype(BF16))
    packed_ref[:, :width] = normed
    packed_ref[:, width : width + LANES - offset] = tail[:, offset:].astype(BF16)


def normalize(residual, mine, other, routing, router):
    steps, rows, width = residual.shape
    count = steps * rows
    padded = -(-(width + 2 * EXPERTS) // LANES) * LANES
    return pl.pallas_call(
        norm_kernel,
        out_shape=(vmem((count, width), F32), vmem((count, padded), BF16)),
        in_specs=whole(5),
        out_specs=whole(2),
        compiler_params=params(),
        name="normalize",
    )(held(residual), held(mine), held(other), held(routing), held(router.T))


def weights_kernel(step, packed_ref, mantissa_hbm, exponent_ref, *refs):
    out_refs, (power, expander, sems) = refs[:-3], refs[-3:]
    units, blocks = power.shape
    width = expander.shape[1]
    pieces = [(part, first) for part in range(len(out_refs)) for first in range(0, units, step)]
    moves = [
        pltpu.make_async_copy(
            mantissa_hbm.at[part, pl.ds(first, step), :], out_refs[part].at[pl.ds(first, step), :], sems.at[place]
        )
        for place, (part, first) in enumerate(pieces)
    ]
    for move in moves[:AHEAD]:
        move.start()
    expander[...] = (iota((blocks, width), 1) // BLOCK == iota((blocks, width), 0)).astype(BF16)
    for place, (part, first) in enumerate(pieces):
        if first == 0:
            exponent = exponent_ref[part * blocks : (part + 1) * blocks, 0, :]
            power[...] = jnp.exp2(exponent.astype(F32)).T.astype(BF16)
        rows = slice(first, first + step)
        moves[place].wait()
        for move in moves[place + AHEAD : place + AHEAD + 1]:
            move.start()
        scale = dot(power[rows, :], expander[...])
        out_refs[part][rows, :] = (out_refs[part][rows, :].astype(F32) * scale).astype(BF16)


def dequantize(packed, mantissa, exponent):
    parts, units, width = mantissa.shape
    blocks = exponent.shape[0] // parts
    step = unit_step(units)
    return pl.pallas_call(
        functools.partial(weights_kernel, step),
        out_shape=(vmem((units, width), BF16),) * parts,
        in_specs=[whole(1)[0], pl.BlockSpec(memory_space=pltpu.HBM), whole(1)[0]],
        out_specs=whole(parts),
        scratch_shapes=[
            pltpu.VMEM((units, blocks), BF16),
            pltpu.VMEM((blocks, width), BF16),
            pltpu.SemaphoreType.DMA((parts * units // step,)),
        ],
        compiler_params=params(14),
        cost_estimate=pl.CostEstimate(
            flops=2 * parts * units * blocks * width, bytes_accessed=2 * parts * units * width, transcendentals=0
        ),
        name="weights",
    )(held(packed), afar(mantissa), held(exponent))


def experts_kernel(gate_ref, up_ref, down_ref, member_ref, *refs):
    arrived, (mine_ref, other_ref, rows, share) = refs[:-4], refs[-4:]
    units, width = gate_ref.shape
    place = 0
    for ref in arrived:
        rows[place : place + ref.shape[0], :] = ref[...]
        place += ref.shape[0]
    inputs = rows[:, :width]
    high = rows[:, width : width + EXPERTS]
    low = rows[:, width + EXPERTS : width + 2 * EXPERTS]
    share[...] = dot(member_ref[...], high, TT) + dot(member_ref[...], low, TT)
    step = unit_step(units)
    hidden = []
    for first in range(0, units, step):
        here = slice(first, first + step)
        gate = dot(gate_ref[here, :], inputs, NT)
        up = dot(up_ref[here, :], inputs, NT)
        hidden.append((gate * jax.nn.sigmoid(gate) * up * share[here, :]).astype(BF16))
    hidden = jnp.concatenate(hidden, axis=0).T
    half = mine_ref.shape[0]
    for first in range(0, width, 512):
        here = slice(first, min(first + 512, width))
        total = dot(hidden, down_ref[:, here])
        mine_ref[:, here] = total[:half, :]
        other_ref[:, here] = total[half:, :].astype(BF16)


def unit_step(units):
    for step in range(240, 15, -16):
        if units % step == 0:
            return step
    return units


def run_experts(weights, member, arrived):
    units, width = weights[0].shape
    count = sum(block.shape[0] for block in arrived)
    padded = arrived[0].shape[1]
    return pl.pallas_call(
        experts_kernel,
        out_shape=(vmem((count // 2, width), F32), vmem((count // 2, width), BF16)),
        in_specs=whole(4 + len(arrived)),
        out_specs=whole(2),
        scratch_shapes=[pltpu.VMEM((count, padded), BF16), pltpu.VMEM((units, count), F32)],
        compiler_params=params(16),
        cost_estimate=pl.CostEstimate(
            flops=6 * count * units * width, bytes_accessed=6 * units * width, transcendentals=0
        ),
        name="experts",
    )(*[held(kind) for kind in weights], held(member), *[held(block) for block in arrived])


def join_kernel(mine_ref, other_ref, *out_refs):
    count = out_refs[0].shape[0]
    for turn, out_ref in enumerate(out_refs):
        here = slice(turn * count, (turn + 1) * count)
        out_ref[...] = (mine_ref[here, :] + other_ref[here, :].astype(F32)).astype(BF16)


def join(mine, other, count):
    turns = mine.shape[0] // count
    return pl.pallas_call(
        join_kernel,
        out_shape=[vmem((count, mine.shape[1]), BF16)] * turns,
        in_specs=whole(2),
        out_specs=whole(turns),
        compiler_params=params(),
        name="join",
    )(held(mine), held(other))


def last_kernel(mixed_ref, mine_ref, other_ref, out_ref):
    steps, rows, _ = out_ref.shape
    result = (mixed_ref[...] + (mine_ref[...] + other_ref[...])).astype(BF16)
    for step in range(steps):
        out_ref[step] = result[step * rows : (step + 1) * rows, :]


def last(mixed, mine, other, shape):
    return pl.pallas_call(
        last_kernel,
        out_shape=jax.ShapeDtypeStruct(shape, BF16),
        in_specs=whole(3),
        out_specs=pl.BlockSpec(memory_space=pltpu.VMEM),
        compiler_params=params(),
        name="last",
    )(held(mixed), held(mine), held(other))


def swap(value):
    return lax.ppermute(value, "tensor", [(0, 1), (1, 0)])


def partners(count):
    half = count // 2
    power = count & (count - 1) == 0
    reach = lambda place, far: place ^ far if power else (place + far) % count
    turns = []
    for turn in range(half):
        pairs = []
        for place in range(count):
            pairs.append((2 * place, 2 * reach(place, turn)))
            pairs.append((2 * place + 1, 2 * reach(place, turn + half) + 1))
        turns.append(pairs)
    return turns


def per_device(residual, queries, new_kv, cache_kv, lengths, routing, router, out_proj, mantissa, exponent, placement):
    places = lax.axis_size("expert")
    place = lax.axis_index("expert")
    steps, rows, width = residual.shape
    count = steps * rows
    units = mantissa.shape[1]
    turns = partners(places)
    both = ("expert", "tensor")

    partial = attend(lengths, queries, new_kv, cache_kv, out_proj)
    mantissa = mantissa[0].transpose(1, 0, 2)
    exponent = exponent.transpose(2, 3, 0, 1).reshape(-1, 1, units)
    tile = place * (units // TILE_UNITS) + jnp.arange(units) // TILE_UNITS
    member = jnp.any(placement.reshape(EXPERTS, -1, 1) == tile, axis=1).astype(BF16)

    mixed, packed = normalize(residual, partial, swap(partial), routing.reshape(count, TOP), router)
    near = [lax.ppermute(packed, both, pairs) for pairs in turns]
    weights = dequantize(packed, mantissa, exponent)
    near, weights = lax.optimization_barrier((near, weights))
    far = [swap(block) for block in near]
    mine, other = run_experts(weights, member, near + far)
    sums = join(mine, swap(other), count)
    back = [
        lax.ppermute(block, both, [(to, back) for back, to in pairs]) for block, pairs in zip(sums, turns)
    ]
    total = sum(block.astype(F32) for block in back)
    return last(mixed, total, swap(total), residual.shape)


def solution(mesh):
    placed = (
        P(None, ("group", "expert"), None),
        P(None, ("group", "expert"), "tensor"),
        P(None, ("group", "expert"), None, "tensor"),
        P(("group", "expert"), None, None, "tensor"),
        P(("group", "expert")),
        P(None, ("group", "expert"), None),
        P(),
        P("tensor", None),
        P("tensor", "expert", None, None),
        P("tensor", "expert", None, None),
        P("group"),
    )
    return jax.shard_map(
        per_device,
        mesh=mesh,
        in_specs=placed,
        out_specs=P(None, ("group", "expert"), None),
        check_vma=False,
    )
```

```python
import functools

import jax
import jax.numpy as jnp
from jax import lax
from jax.experimental import pallas as pl
from jax.experimental.pallas import tpu as pltpu
from jax.sharding import PartitionSpec as P

HD = 64
EXPERTS = 8
TOP = 4
BLOCK = 32
TILE_UNITS = 6
LANES = 128
AHEAD = 3
F32 = jnp.float32
BF16 = jnp.bfloat16

NT = (((1,), (1,)), ((), ()))
TN = (((0,), (0,)), ((), ()))
TT = (((0,), (1,)), ((), ()))


def dot(a, b, dims=(((1,), (0,)), ((), ()))):
    return lax.dot_general(a, b, dims, preferred_element_type=F32)


def iota(shape, dim):
    return lax.broadcasted_iota(jnp.int32, shape, dim)


def vmem(shape, dtype):
    return pltpu.VMEM(shape, dtype)


def held(value):
    return pltpu.with_memory_space_constraint(value, pltpu.VMEM)


def afar(value):
    return pltpu.with_memory_space_constraint(value, pltpu.HBM)


def whole(count):
    return [pl.BlockSpec(memory_space=pltpu.VMEM)] * count


def params(mebibytes=8):
    return pltpu.CompilerParams(vmem_limit_bytes=mebibytes << 20)


def attention_kernel(
    lengths_hbm,
    queries_hbm,
    fresh_hbm,
    cache_hbm,
    proj_hbm,
    out_ref,
    lengths,
    queries,
    fresh_rows,
    cache_rows,
    proj,
    spread,
    packed,
    mixed,
    sems,
):
    moves = [
        pltpu.make_async_copy(source, target, sems.at[place])
        for place, (source, target) in enumerate(
            (
                (queries_hbm, queries),
                (lengths_hbm, lengths),
                (fresh_hbm, fresh_rows),
                (cache_hbm, cache_rows),
                (proj_hbm, proj),
            )
        )
    ]
    for move in moves:
        move.start()
    steps, rows, _ = queries.shape
    count = steps * rows
    groups = queries.shape[2] // LANES
    half = groups // 2
    lane = iota((rows, LANES), 1)
    moves[0].wait()
    for step in range(steps):
        for group in range(groups):
            piece = queries[step, :, group * LANES : (group + 1) * LANES].astype(F32) * (HD**-0.5)
            mine = (lane < HD) == (group < half)
            first = group * count + step * rows
            packed[first : first + rows, :] = jnp.where(mine, piece, 0.0)
            first += groups * count
            packed[first : first + rows, :] = jnp.where(mine, pltpu.roll(piece, HD, 1), 0.0)
    amount = 2 * groups * steps
    span = cache_rows.shape[1] // 2
    spot = iota((amount, span), 1)
    step_of = iota((amount, count), 0) % steps
    fresh_spot = iota((amount, count), 1)
    for move in moves[1:4]:
        move.wait()

    def apart(value, which):
        size = value.shape[0]
        here = spread.at[which, :size]
        here[...] = value.astype(F32)
        return tuple(
            spread[which, pl.ds(first, size // 2, stride=2), :].astype(BF16) for first in range(2)
        )

    fresh_keys, fresh_values = apart(fresh_rows[...], rows)
    for row in range(rows):
        now = packed[pl.ds(row, amount, stride=rows), :].astype(BF16)
        keys, values = apart(cache_rows[row], row)
        scores = jnp.where(spot < lengths[row], dot(now, keys, NT), -1e30)
        seen = (fresh_spot % rows == row) & (fresh_spot // rows <= step_of)
        late = jnp.where(seen, dot(now, fresh_keys, NT), -1e30)
        highest = jnp.maximum(
            jnp.max(scores, axis=1, keepdims=True), jnp.max(late, axis=1, keepdims=True)
        )
        scores = jnp.exp(scores - highest)
        late = jnp.exp(late - highest)
        total = jnp.sum(scores, axis=1, keepdims=True) + jnp.sum(late, axis=1, keepdims=True)
        probs = (scores / total).astype(BF16)
        late_probs = (late / total).astype(BF16)
        mixed[pl.ds(row, amount, stride=rows), :] = dot(probs, values) + dot(late_probs, fresh_values)
    heads = []
    lane = iota((count, LANES), 1)
    for group in range(groups):
        straight = mixed[group * count : (group + 1) * count, :]
        turned = mixed[(groups + group) * count : (groups + group + 1) * count, :]
        mine = (lane < HD) == (group < half)
        heads.append(jnp.where(mine, straight, pltpu.roll(turned, HD, 1)).astype(BF16))
    moves[4].wait()
    out_ref[...] = dot(jnp.concatenate(heads, axis=1), proj[...], NT)


def attend(lengths, queries, new_kv, cache_kv, out_proj):
    steps, rows, width = queries.shape
    span = cache_kv.shape[1]
    proj = out_proj.T
    model_width = proj.shape[0]
    count = steps * rows
    groups = width // LANES
    fresh = new_kv.reshape(count * 2, LANES)
    cache = cache_kv.reshape(rows, 2 * span, LANES)
    return pl.pallas_call(
        attention_kernel,
        out_shape=vmem((count, model_width), F32),
        in_specs=[pl.BlockSpec(memory_space=pltpu.HBM)] * 5,
        out_specs=pl.BlockSpec(memory_space=pltpu.VMEM),
        scratch_shapes=[
            pltpu.SMEM(lengths.shape, jnp.int32),
            pltpu.VMEM(queries.shape, BF16),
            pltpu.VMEM(fresh.shape, BF16),
            pltpu.VMEM(cache.shape, BF16),
            pltpu.VMEM(proj.shape, BF16),
            pltpu.VMEM((rows + 1, 2 * span, LANES), F32),
            pltpu.VMEM((2 * groups * count, LANES), F32),
            pltpu.VMEM((2 * groups * count, LANES), F32),
            pltpu.SemaphoreType.DMA((5,)),
        ],
        compiler_params=params(16),
        cost_estimate=pl.CostEstimate(
            flops=2 * count * width * model_width, bytes_accessed=7 << 20, transcendentals=0
        ),
        name="attention",
    )(afar(lengths), afar(queries), afar(fresh), afar(cache), afar(proj))


def norm_kernel(residual_ref, mine_ref, other_ref, routing_ref, router_ref, mixed_ref, packed_ref):
    steps, rows, width = residual_ref.shape
    for step in range(steps):
        mixed_ref[step * rows : (step + 1) * rows, :] = residual_ref[step].astype(F32)
    mixed = mixed_ref[...] + (mine_ref[...] + other_ref[...])
    mixed_ref[...] = mixed
    scale = lax.rsqrt(jnp.mean(mixed * mixed, axis=1, keepdims=True) + 1e-05)
    normed = (mixed * scale).astype(BF16)
    logits = dot(normed, router_ref[...], NT)
    routing = routing_ref[...]
    expert = iota(logits.shape, 1)
    chosen = expert == routing[:, 0:1]
    for slot in range(1, TOP):
        chosen = chosen | (expert == routing[:, slot : slot + 1])
    sigmoids = jnp.where(chosen, jax.nn.sigmoid(logits), 0.0)
    gates = sigmoids / jnp.sum(sigmoids, axis=1, keepdims=True)
    high = gates.astype(BF16)
    low = (gates - high.astype(F32)).astype(BF16)
    first = width // LANES * LANES
    offset = width - first
    target = iota((EXPERTS, LANES), 1) - iota((EXPERTS, LANES), 0)
    tail = dot(high, (target == offset).astype(BF16)) + dot(low, (target == offset + EXPERTS).astype(BF16))
    packed_ref[:, :width] = normed
    packed_ref[:, width : width + LANES - offset] = tail[:, offset:].astype(BF16)


def normalize(residual, mine, other, routing, router):
    steps, rows, width = residual.shape
    count = steps * rows
    padded = -(-(width + 2 * EXPERTS) // LANES) * LANES
    return pl.pallas_call(
        norm_kernel,
        out_shape=(vmem((count, width), F32), vmem((count, padded), BF16)),
        in_specs=whole(5),
        out_specs=whole(2),
        compiler_params=params(),
        name="normalize",
    )(held(residual), held(mine), held(other), held(routing), held(router.T))


def weights_kernel(step, packed_ref, mantissa_hbm, exponent_ref, *refs):
    out_refs, (power, expander, sems) = refs[:-3], refs[-3:]
    units, blocks = power.shape
    width = expander.shape[1]
    pieces = [(part, first) for part in range(len(out_refs)) for first in range(0, units, step)]
    moves = [
        pltpu.make_async_copy(
            mantissa_hbm.at[part, pl.ds(first, step), :], out_refs[part].at[pl.ds(first, step), :], sems.at[place]
        )
        for place, (part, first) in enumerate(pieces)
    ]
    for move in moves[:AHEAD]:
        move.start()
    expander[...] = (iota((blocks, width), 1) // BLOCK == iota((blocks, width), 0)).astype(BF16)
    for place, (part, first) in enumerate(pieces):
        if first == 0:
            exponent = exponent_ref[part * blocks : (part + 1) * blocks, 0, :]
            power[...] = jnp.exp2(exponent.astype(F32)).T.astype(BF16)
        rows = slice(first, first + step)
        moves[place].wait()
        for move in moves[place + AHEAD : place + AHEAD + 1]:
            move.start()
        scale = dot(power[rows, :], expander[...])
        out_refs[part][rows, :] = (out_refs[part][rows, :].astype(F32) * scale).astype(BF16)


def dequantize(packed, mantissa, exponent):
    parts, units, width = mantissa.shape
    blocks = exponent.shape[0] // parts
    step = unit_step(units)
    return pl.pallas_call(
        functools.partial(weights_kernel, step),
        out_shape=(vmem((units, width), BF16),) * parts,
        in_specs=[whole(1)[0], pl.BlockSpec(memory_space=pltpu.HBM), whole(1)[0]],
        out_specs=whole(parts),
        scratch_shapes=[
            pltpu.VMEM((units, blocks), BF16),
            pltpu.VMEM((blocks, width), BF16),
            pltpu.SemaphoreType.DMA((parts * units // step,)),
        ],
        compiler_params=params(14),
        cost_estimate=pl.CostEstimate(flops=1000, bytes_accessed=1000, transcendentals=0),
        name="weights",
    )(held(packed), afar(mantissa), held(exponent))


def experts_kernel(gate_ref, up_ref, down_ref, member_ref, *refs):
    arrived, (mine_ref, other_ref, rows, share) = refs[:-4], refs[-4:]
    units, width = gate_ref.shape
    place = 0
    for ref in arrived:
        rows[place : place + ref.shape[0], :] = ref[...]
        place += ref.shape[0]
    inputs = rows[:, :width]
    high = rows[:, width : width + EXPERTS]
    low = rows[:, width + EXPERTS : width + 2 * EXPERTS]
    share[...] = dot(member_ref[...], high, TT) + dot(member_ref[...], low, TT)
    step = unit_step(units)
    hidden = []
    for first in range(0, units, step):
        here = slice(first, first + step)
        gate = dot(gate_ref[here, :], inputs, NT)
        up = dot(up_ref[here, :], inputs, NT)
        hidden.append((gate * jax.nn.sigmoid(gate) * up * share[here, :]).astype(BF16))
    hidden = jnp.concatenate(hidden, axis=0).T
    half = mine_ref.shape[0]
    for first in range(0, width, 512):
        here = slice(first, min(first + 512, width))
        total = dot(hidden, down_ref[:, here])
        mine_ref[:, here] = total[:half, :]
        other_ref[:, here] = total[half:, :].astype(BF16)


def unit_step(units):
    for step in range(240, 15, -16):
        if units % step == 0:
            return step
    return units


def run_experts(weights, member, arrived):
    units, width = weights[0].shape
    count = sum(block.shape[0] for block in arrived)
    padded = arrived[0].shape[1]
    return pl.pallas_call(
        experts_kernel,
        out_shape=(vmem((count // 2, width), F32), vmem((count // 2, width), BF16)),
        in_specs=whole(4 + len(arrived)),
        out_specs=whole(2),
        scratch_shapes=[pltpu.VMEM((count, padded), BF16), pltpu.VMEM((units, count), F32)],
        compiler_params=params(16),
        cost_estimate=pl.CostEstimate(
            flops=6 * count * units * width, bytes_accessed=6 * units * width, transcendentals=0
        ),
        name="experts",
    )(*[held(kind) for kind in weights], held(member), *[held(block) for block in arrived])


def join_kernel(mine_ref, other_ref, *out_refs):
    count = out_refs[0].shape[0]
    for turn, out_ref in enumerate(out_refs):
        here = slice(turn * count, (turn + 1) * count)
        out_ref[...] = (mine_ref[here, :] + other_ref[here, :].astype(F32)).astype(BF16)


def join(mine, other, count):
    turns = mine.shape[0] // count
    return pl.pallas_call(
        join_kernel,
        out_shape=[vmem((count, mine.shape[1]), BF16)] * turns,
        in_specs=whole(2),
        out_specs=whole(turns),
        compiler_params=params(),
        name="join",
    )(held(mine), held(other))


def last_kernel(mixed_ref, mine_ref, other_ref, out_ref):
    steps, rows, _ = out_ref.shape
    result = (mixed_ref[...] + (mine_ref[...] + other_ref[...])).astype(BF16)
    for step in range(steps):
        out_ref[step] = result[step * rows : (step + 1) * rows, :]


def last(mixed, mine, other, shape):
    return pl.pallas_call(
        last_kernel,
        out_shape=jax.ShapeDtypeStruct(shape, BF16),
        in_specs=whole(3),
        out_specs=pl.BlockSpec(memory_space=pltpu.VMEM),
        compiler_params=params(),
        name="last",
    )(held(mixed), held(mine), held(other))


def swap(value):
    return lax.ppermute(value, "tensor", [(0, 1), (1, 0)])


def partners(count):
    power = count & (count - 1) == 0
    reach = lambda place, far: place ^ far if power else (place + far) % count
    far = sorted(range(count), key=lambda k: (k.bit_count() % 2, -k))
    half = count // 2
    return [
        [(2 * place + core, 2 * reach(place, far[turn + core * half]) + core) for place in range(count) for core in range(2)]
        for turn in range(half)
    ]


def per_device(residual, queries, new_kv, cache_kv, lengths, routing, router, out_proj, mantissa, exponent, placement):
    places = lax.axis_size("expert")
    place = lax.axis_index("expert")
    steps, rows, width = residual.shape
    count = steps * rows
    units = mantissa.shape[1]
    turns = partners(places)
    both = ("expert", "tensor")

    partial = attend(lengths, queries, new_kv, cache_kv, out_proj)
    mantissa = mantissa[0].transpose(1, 0, 2)
    exponent = exponent.transpose(2, 3, 0, 1).reshape(-1, 1, units)
    tile = place * (units // TILE_UNITS) + jnp.arange(units) // TILE_UNITS
    member = jnp.any(placement.reshape(EXPERTS, -1, 1) == tile, axis=1).astype(BF16)

    mixed, packed = normalize(residual, partial, swap(partial), routing.reshape(count, TOP), router)
    near = [lax.ppermute(packed, both, pairs) for pairs in turns]
    weights = dequantize(packed, mantissa, exponent)
    near, weights = lax.optimization_barrier((near[::-1], weights))
    near = near[::-1]
    far = [swap(block) for block in near]
    mine, other = run_experts(weights, member, near + far)
    sums = join(mine, swap(other), count)
    back = [
        lax.ppermute(block, both, [(to, back) for back, to in pairs]) for block, pairs in zip(sums, turns)
    ]
    total = sum(block.astype(F32) for block in back)
    return last(mixed, total, swap(total), residual.shape)


def solution(mesh):
    placed = (
        P(None, ("group", "expert"), None),
        P(None, ("group", "expert"), "tensor"),
        P(None, ("group", "expert"), None, "tensor"),
        P(("group", "expert"), None, None, "tensor"),
        P(("group", "expert")),
        P(None, ("group", "expert"), None),
        P(),
        P("tensor", None),
        P("tensor", "expert", None, None),
        P("tensor", "expert", None, None),
        P("group"),
    )
    return jax.shard_map(
        per_device,
        mesh=mesh,
        in_specs=placed,
        out_specs=P(None, ("group", "expert"), None),
        check_vma=False,
    )
```

```python
import functools

import jax
import jax.numpy as jnp
from jax import lax
from jax.experimental import pallas as pl
from jax.experimental.pallas import tpu as pltpu
from jax.sharding import PartitionSpec as P

HD = 64
EXPERTS = 8
TOP = 4
BLOCK = 32
TILE_UNITS = 6
LANES = 128
AHEAD = 3
F32 = jnp.float32
BF16 = jnp.bfloat16

NT = (((1,), (1,)), ((), ()))


def dot(a, b, dims=(((1,), (0,)), ((), ()))):
    return lax.dot_general(a, b, dims, preferred_element_type=F32)


def iota(shape, dim):
    return lax.broadcasted_iota(jnp.int32, shape, dim)


def vmem(shape, dtype):
    return pltpu.VMEM(shape, dtype)


def held(value):
    return pltpu.with_memory_space_constraint(value, pltpu.VMEM)


def afar(value):
    return pltpu.with_memory_space_constraint(value, pltpu.HBM)


def whole(count):
    return [pl.BlockSpec(memory_space=pltpu.VMEM)] * count


def params(mebibytes=8):
    return pltpu.CompilerParams(vmem_limit_bytes=mebibytes << 20)


def attention_kernel(
    lengths_hbm,
    queries_hbm,
    fresh_hbm,
    cache_hbm,
    proj_hbm,
    out_ref,
    lengths,
    queries,
    fresh_rows,
    cache_rows,
    proj,
    spread,
    packed,
    mixed,
    sems,
):
    moves = [
        pltpu.make_async_copy(source, target, sems.at[place])
        for place, (source, target) in enumerate(
            (
                (queries_hbm, queries),
                (lengths_hbm, lengths),
                (fresh_hbm, fresh_rows),
                (cache_hbm, cache_rows),
                (proj_hbm, proj),
            )
        )
    ]
    for move in moves:
        move.start()
    steps, rows, _ = queries.shape
    count = steps * rows
    groups = queries.shape[2] // LANES
    half = groups // 2
    lane = iota((rows, LANES), 1)
    moves[0].wait()
    for step in range(steps):
        for group in range(groups):
            piece = queries[step, :, group * LANES : (group + 1) * LANES].astype(F32) * (HD**-0.5)
            mine = (lane < HD) == (group < half)
            first = group * count + step * rows
            packed[first : first + rows, :] = jnp.where(mine, piece, 0.0)
            first += groups * count
            packed[first : first + rows, :] = jnp.where(mine, pltpu.roll(piece, HD, 1), 0.0)
    amount = 2 * groups * steps
    span = cache_rows.shape[1] // 2
    spot = iota((amount, span), 1)
    step_of = iota((amount, count), 0) % steps
    fresh_spot = iota((amount, count), 1)
    for move in moves[1:4]:
        move.wait()

    def apart(value, which):
        size = value.shape[0]
        here = spread.at[which, :size]
        here[...] = value.astype(F32)
        return tuple(
            spread[which, pl.ds(first, size // 2, stride=2), :].astype(BF16) for first in range(2)
        )

    fresh_keys, fresh_values = apart(fresh_rows[...], rows)
    for row in range(rows):
        now = packed[pl.ds(row, amount, stride=rows), :].astype(BF16)
        keys, values = apart(cache_rows[row], row)
        scores = jnp.where(spot < lengths[row], dot(now, keys, NT), -1e30)
        seen = (fresh_spot % rows == row) & (fresh_spot // rows <= step_of)
        late = jnp.where(seen, dot(now, fresh_keys, NT), -1e30)
        highest = jnp.maximum(
            jnp.max(scores, axis=1, keepdims=True), jnp.max(late, axis=1, keepdims=True)
        )
        scores = jnp.exp(scores - highest)
        late = jnp.exp(late - highest)
        total = jnp.sum(scores, axis=1, keepdims=True) + jnp.sum(late, axis=1, keepdims=True)
        probs = (scores / total).astype(BF16)
        late_probs = (late / total).astype(BF16)
        mixed[pl.ds(row, amount, stride=rows), :] = dot(probs, values) + dot(late_probs, fresh_values)
    heads = []
    lane = iota((count, LANES), 1)
    for group in range(groups):
        straight = mixed[group * count : (group + 1) * count, :]
        turned = mixed[(groups + group) * count : (groups + group + 1) * count, :]
        mine = (lane < HD) == (group < half)
        heads.append(jnp.where(mine, straight, pltpu.roll(turned, HD, 1)).astype(BF16))
    moves[4].wait()
    out_ref[...] = dot(jnp.concatenate(heads, axis=1), proj[...], NT)


def attend(lengths, queries, new_kv, cache_kv, out_proj):
    steps, rows, width = queries.shape
    span = cache_kv.shape[1]
    proj = out_proj.T
    model_width = proj.shape[0]
    count = steps * rows
    groups = width // LANES
    fresh = new_kv.reshape(count * 2, LANES)
    cache = cache_kv.reshape(rows, 2 * span, LANES)
    return pl.pallas_call(
        attention_kernel,
        out_shape=vmem((count, model_width), F32),
        in_specs=[pl.BlockSpec(memory_space=pltpu.HBM)] * 5,
        out_specs=pl.BlockSpec(memory_space=pltpu.VMEM),
        scratch_shapes=[
            pltpu.SMEM(lengths.shape, jnp.int32),
            pltpu.VMEM(queries.shape, BF16),
            pltpu.VMEM(fresh.shape, BF16),
            pltpu.VMEM(cache.shape, BF16),
            pltpu.VMEM(proj.shape, BF16),
            pltpu.VMEM((rows + 1, 2 * span, LANES), F32),
            pltpu.VMEM((2 * groups * count, LANES), F32),
            pltpu.VMEM((2 * groups * count, LANES), F32),
            pltpu.SemaphoreType.DMA((5,)),
        ],
        compiler_params=params(16),
        cost_estimate=pl.CostEstimate(
            flops=2 * count * width * model_width, bytes_accessed=7 << 20, transcendentals=0
        ),
        name="attention",
    )(afar(lengths), afar(queries), afar(fresh), afar(cache), afar(proj))


def norm_kernel(residual_ref, mine_ref, other_ref, routing_ref, router_ref, mixed_ref, packed_ref):
    steps, rows, width = residual_ref.shape
    for step in range(steps):
        mixed_ref[step * rows : (step + 1) * rows, :] = residual_ref[step].astype(F32)
    mixed = mixed_ref[...] + (mine_ref[...] + other_ref[...])
    mixed_ref[...] = mixed
    scale = lax.rsqrt(jnp.mean(mixed * mixed, axis=1, keepdims=True) + 1e-05)
    normed = (mixed * scale).astype(BF16)
    logits = dot(normed, router_ref[...], NT)
    routing = routing_ref[...]
    expert = iota(logits.shape, 1)
    chosen = expert == routing[:, 0:1]
    for slot in range(1, TOP):
        chosen = chosen | (expert == routing[:, slot : slot + 1])
    sigmoids = jnp.where(chosen, jax.nn.sigmoid(logits), 0.0)
    gates = sigmoids / jnp.sum(sigmoids, axis=1, keepdims=True)
    high = gates.astype(BF16)
    low = (gates - high.astype(F32)).astype(BF16)
    first = width // LANES * LANES
    offset = width - first
    target = iota((EXPERTS, LANES), 1) - iota((EXPERTS, LANES), 0)
    tail = dot(high, (target == offset).astype(BF16)) + dot(low, (target == offset + EXPERTS).astype(BF16))
    packed_ref[:, :width] = normed
    packed_ref[:, width : width + LANES - offset] = tail[:, offset:].astype(BF16)


def normalize(residual, mine, other, routing, router):
    steps, rows, width = residual.shape
    count = steps * rows
    padded = -(-(width + 2 * EXPERTS) // LANES) * LANES
    return pl.pallas_call(
        norm_kernel,
        out_shape=(vmem((count, width), F32), vmem((count, padded), BF16)),
        in_specs=whole(5),
        out_specs=whole(2),
        compiler_params=params(),
        name="normalize",
    )(held(residual), held(mine), held(other), held(routing), held(router.T))


def weights_kernel(step, rows_ref, mantissa_hbm, exponent_ref, placement_ref, *refs):
    out_refs, member_ref, (power, expander, sems) = refs[:-4], refs[-4], refs[-3:]
    units, blocks = power.shape
    width = expander.shape[1]
    pieces = [(part, first) for part in range(len(out_refs)) for first in range(0, units, step)]
    moves = [
        pltpu.make_async_copy(
            mantissa_hbm.at[part, pl.ds(first, step), :], out_refs[part].at[pl.ds(first, step), :], sems.at[place]
        )
        for place, (part, first) in enumerate(pieces)
    ]
    for move in moves[:AHEAD]:
        move.start()

    experts, slots = placement_ref.shape
    tiles = units // TILE_UNITS
    tile = lax.axis_index("expert") * tiles + iota((tiles, slots), 0)
    lane = iota((slots, LANES), 1) - width % LANES
    found = jnp.zeros((tiles, LANES), F32)
    for expert in range(experts):
        here = (placement_ref[expert : expert + 1, :] == tile).astype(BF16)
        found += dot(here, ((lane == expert) | (lane == expert + experts)).astype(BF16))
    spread = (iota((units, tiles), 0) // TILE_UNITS == iota((units, tiles), 1)).astype(BF16)
    member_ref[...] = dot(spread, found.astype(BF16)).astype(BF16)

    expander[...] = (iota((blocks, width), 1) // BLOCK == iota((blocks, width), 0)).astype(BF16)
    for place, (part, first) in enumerate(pieces):
        if first == 0:
            exponent = exponent_ref[part * blocks : (part + 1) * blocks, 0, :]
            power[...] = jnp.exp2(exponent.astype(F32)).T.astype(BF16)
        rows = slice(first, first + step)
        moves[place].wait()
        for move in moves[place + AHEAD : place + AHEAD + 1]:
            move.start()
        scale = dot(power[rows, :], expander[...])
        out_refs[part][rows, :] = (out_refs[part][rows, :].astype(F32) * scale).astype(BF16)


def dequantize(rows, mantissa, exponent, placement):
    parts, units, width = mantissa.shape
    blocks = exponent.shape[0] // parts
    step = unit_step(units)
    *weights, member = pl.pallas_call(
        functools.partial(weights_kernel, step),
        out_shape=(vmem((units, width), BF16),) * parts + (vmem((units, LANES), BF16),),
        in_specs=whole(1) + [pl.BlockSpec(memory_space=pltpu.HBM)] + whole(2),
        out_specs=whole(parts + 1),
        scratch_shapes=[
            pltpu.VMEM((units, blocks), BF16),
            pltpu.VMEM((blocks, width), BF16),
            pltpu.SemaphoreType.DMA((parts * units // step,)),
        ],
        compiler_params=params(14),
        cost_estimate=pl.CostEstimate(flops=1000, bytes_accessed=1000, transcendentals=0),
        name="weights",
    )(held(rows), afar(mantissa), held(exponent), held(placement))
    return weights, member


def experts_kernel(gate_ref, up_ref, down_ref, member_ref, *refs):
    arrived, (mine_ref, other_ref, rows) = refs[:-3], refs[-3:]
    units, width = gate_ref.shape
    place = 0
    for ref in arrived:
        rows[place : place + ref.shape[0], :] = ref[...]
        place += ref.shape[0]
    inputs = rows[:, :width]
    gates = rows[:, rows.shape[1] - LANES :]
    step = unit_step(units)
    hidden = []
    for first in range(0, units, step):
        here = slice(first, first + step)
        gate = dot(gate_ref[here, :], inputs, NT)
        up = dot(up_ref[here, :], inputs, NT)
        share = dot(member_ref[here, :], gates, NT)
        hidden.append((gate * jax.nn.sigmoid(gate) * up * share).astype(BF16))
    hidden = jnp.concatenate(hidden, axis=0).T
    half = mine_ref.shape[0]
    for first in range(0, width, 512):
        here = slice(first, min(first + 512, width))
        total = dot(hidden, down_ref[:, here])
        mine_ref[:, here] = total[:half, :]
        other_ref[:, here] = total[half:, :].astype(BF16)


def unit_step(units):
    for step in range(240, 15, -16):
        if units % step == 0:
            return step
    return units


def run_experts(weights, member, arrived):
    units, width = weights[0].shape
    count = sum(block.shape[0] for block in arrived)
    padded = arrived[0].shape[1]
    return pl.pallas_call(
        experts_kernel,
        out_shape=(vmem((count // 2, width), F32), vmem((count // 2, width), BF16)),
        in_specs=whole(4 + len(arrived)),
        out_specs=whole(2),
        scratch_shapes=[pltpu.VMEM((count, padded), BF16)],
        compiler_params=params(16),
        cost_estimate=pl.CostEstimate(
            flops=6 * count * units * width, bytes_accessed=6 * units * width, transcendentals=0
        ),
        name="experts",
    )(*[held(kind) for kind in weights], held(member), *[held(block) for block in arrived])


def local(kernel, name, shapes, *values):
    return pl.pallas_call(
        kernel,
        out_shape=[vmem(*shape) for shape in shapes],
        in_specs=whole(len(values)),
        out_specs=whole(len(shapes)),
        compiler_params=params(),
        name=name,
    )(*[held(value) for value in values])


def join_kernel(mine_ref, other_ref, *out_refs):
    count = out_refs[0].shape[0]
    for turn, out_ref in enumerate(out_refs):
        here = slice(turn * count, (turn + 1) * count)
        out_ref[...] = (mine_ref[here, :] + other_ref[here, :].astype(F32)).astype(out_ref.dtype)


def join(mine, other, count, kept):
    rows, width = mine.shape
    shapes = [((count, width), F32 if turn < kept else BF16) for turn in range(rows // count)]
    return local(join_kernel, "join", shapes, mine, other)


def merge_kernel(mine_ref, other_ref, out_ref):
    out_ref[...] = (mine_ref[...] + other_ref[...].astype(F32)).astype(BF16)


def merge(mine, other):
    return local(merge_kernel, "merge", [(mine.shape, BF16)], mine, other)[0]


def last_kernel(mixed_ref, mine_ref, other_ref, out_ref):
    steps, rows, _ = out_ref.shape
    result = (mixed_ref[...] + (mine_ref[...] + other_ref[...])).astype(BF16)
    for step in range(steps):
        out_ref[step] = result[step * rows : (step + 1) * rows, :]


def last(mixed, mine, other, shape):
    return pl.pallas_call(
        last_kernel,
        out_shape=jax.ShapeDtypeStruct(shape, BF16),
        in_specs=whole(3),
        out_specs=pl.BlockSpec(memory_space=pltpu.VMEM),
        compiler_params=params(),
        name="last",
    )(held(mixed), held(mine), held(other))


def swap(value):
    return lax.ppermute(value, "tensor", [(0, 1), (1, 0)])


def partners(count):
    share = count // 8
    even = list(range(count - 2, count // 2 - 1, -2))
    even = (even[:share], even[share:])
    odd = [[k + 1 for k in core] for core in even]
    near = tuple([k for k in range(count // 2 - 1, -1, -1) if (k + 1) % 4 // 2 == core] for core in range(2))

    def turns(far):
        return [
            [(2 * place + core, 2 * (place ^ far[core][turn]) + core) for place in range(count) for core in range(2)]
            for turn in range(len(far[0]))
        ]

    return turns(even), turns(odd), turns(near)


def per_device(residual, queries, new_kv, cache_kv, lengths, routing, router, out_proj, mantissa, exponent, placement):
    places = lax.axis_size("expert")
    steps, rows, width = residual.shape
    count = steps * rows
    units = mantissa.shape[1]
    even, odd, close = partners(places)
    turns = even + odd + close
    beside = [(2 * spot + core, 2 * (spot ^ 1) + core) for spot in range(places) for core in range(2)]
    both = ("expert", "tensor")

    partial = attend(lengths, queries, new_kv, cache_kv, out_proj)
    mantissa = mantissa[0].transpose(1, 0, 2)
    exponent = exponent.transpose(2, 3, 0, 1).reshape(-1, 1, units)

    mixed, packed = normalize(residual, partial, swap(partial), routing.reshape(count, TOP), router)
    near = [lax.ppermute(packed, both, pairs) for pairs in turns]
    weights, member = dequantize(packed, mantissa, exponent, placement.reshape(EXPERTS, -1))
    near, weights, member = lax.optimization_barrier((near[::-1], weights, member))
    near = near[::-1]
    far = [swap(block) for block in near]
    mine, other = run_experts(weights, member, near + far)
    sums = join(mine, swap(other), count, len(even))
    passed = [lax.ppermute(block, both, beside) for block in sums[len(even) : 2 * len(even)]]
    back = [
        lax.ppermute(block, both, [(to, back) for back, to in pairs])
        for block, pairs in zip(sums[2 * len(even) :], close)
    ]
    back = [
        lax.ppermute(merge(block, extra), both, [(to, back) for back, to in pairs])
        for block, extra, pairs in zip(sums, passed, even)
    ] + back
    total = sum(block.astype(F32) for block in back)
    return last(mixed, total, swap(total), residual.shape)


def solution(mesh):
    placed = (
        P(None, ("group", "expert"), None),
        P(None, ("group", "expert"), "tensor"),
        P(None, ("group", "expert"), None, "tensor"),
        P(("group", "expert"), None, None, "tensor"),
        P(("group", "expert")),
        P(None, ("group", "expert"), None),
        P(),
        P("tensor", None),
        P("tensor", "expert", None, None),
        P("tensor", "expert", None, None),
        P("group"),
    )
    return jax.shard_map(
        per_device,
        mesh=mesh,
        in_specs=placed,
        out_specs=P(None, ("group", "expert"), None),
        check_vma=False,
    )
```

```python
import functools

import jax
import jax.numpy as jnp
from jax import lax
from jax.experimental import pallas as pl
from jax.experimental.pallas import tpu as pltpu
from jax.sharding import PartitionSpec as P

HD = 64
EXPERTS = 8
TOP = 4
BLOCK = 32
TILE_UNITS = 6
LANES = 128
F32 = jnp.float32
BF16 = jnp.bfloat16

NT = (((1,), (1,)), ((), ()))
TN = (((0,), (0,)), ((), ()))


def dot(a, b, dims=(((1,), (0,)), ((), ()))):
    return lax.dot_general(a, b, dims, preferred_element_type=F32)


def iota(shape, dim):
    return lax.broadcasted_iota(jnp.int32, shape, dim)


def vmem(shape, dtype):
    return pltpu.VMEM(shape, dtype)


def held(value):
    return pltpu.with_memory_space_constraint(value, pltpu.VMEM)


def afar(value):
    return pltpu.with_memory_space_constraint(value, pltpu.HBM)


def whole(count):
    return [pl.BlockSpec(memory_space=pltpu.VMEM)] * count


def params(mebibytes=8):
    return pltpu.CompilerParams(vmem_limit_bytes=mebibytes << 20)


def attention_kernel(
    lengths_hbm,
    queries_hbm,
    fresh_hbm,
    cache_hbm,
    proj_hbm,
    out_ref,
    lengths,
    queries,
    fresh_rows,
    cache_rows,
    proj,
    spread,
    packed,
    mixed,
    sems,
):
    moves = [
        pltpu.make_async_copy(source, target, sems.at[place])
        for place, (source, target) in enumerate(
            (
                (queries_hbm, queries),
                (lengths_hbm, lengths),
                (fresh_hbm, fresh_rows),
                (cache_hbm, cache_rows),
            )
        )
    ]
    chunk = proj.shape[0] // 4
    parts = [
        pltpu.make_async_copy(proj_hbm.at[pl.ds(part * chunk, chunk)], proj.at[pl.ds(part * chunk, chunk)], sems.at[4 + part])
        for part in range(4)
    ]
    for move in moves + parts[:2]:
        move.start()
    steps, rows, _ = queries.shape
    count = steps * rows
    groups = queries.shape[2] // LANES
    half = groups // 2
    lane = iota((rows, LANES), 1)
    moves[0].wait()
    for step in range(steps):
        for group in range(groups):
            piece = queries[step, :, group * LANES : (group + 1) * LANES].astype(F32) * (HD**-0.5)
            mine = (lane < HD) == (group < half)
            first = group * count + step * rows
            packed[first : first + rows, :] = jnp.where(mine, piece, 0.0)
            first += groups * count
            packed[first : first + rows, :] = jnp.where(mine, pltpu.roll(piece, HD, 1), 0.0)
    for move in parts[2:2]:
        move.start()
    amount = 2 * groups * steps
    span = cache_rows.shape[1] // 2
    spot = iota((amount, span), 1)
    step_of = iota((amount, count), 0) % steps
    fresh_spot = iota((amount, count), 1)
    for move in moves[1:4]:
        move.wait()
    for move in parts[2:]:
        move.start()

    def apart(value, which):
        size = value.shape[0]
        here = spread.at[which, :size]
        here[...] = value.astype(F32)
        return tuple(
            spread[which, pl.ds(first, size // 2, stride=2), :].astype(BF16) for first in range(2)
        )

    fresh_keys, fresh_values = apart(fresh_rows[...], rows)
    todo = []
    for row in range(rows):
        now = packed[pl.ds(row, amount, stride=rows), :].astype(BF16)
        keys, values = apart(cache_rows[row], row)
        todo.append((row, values, dot(now, keys, NT), dot(now, fresh_keys, NT)))
    probs = []
    for row, values, scores, late in todo:
        scores = jnp.where(spot < lengths[row], scores, -1e30)
        seen = (fresh_spot % rows == row) & (fresh_spot // rows <= step_of)
        late = jnp.where(seen, late, -1e30)
        highest = jnp.maximum(
            jnp.max(scores, axis=1, keepdims=True), jnp.max(late, axis=1, keepdims=True)
        )
        scores = jnp.exp(scores - highest)
        late = jnp.exp(late - highest)
        total = jnp.sum(scores, axis=1, keepdims=True) + jnp.sum(late, axis=1, keepdims=True)
        total = 1.0 / total
        probs.append((row, values, (scores * total).astype(BF16), (late * total).astype(BF16)))
    for row, values, scores, late in probs:
        mixed[pl.ds(row, amount, stride=rows), :] = dot(scores, values) + dot(late, fresh_values)
    heads = []
    lane = iota((count, LANES), 1)
    for group in range(groups):
        straight = mixed[group * count : (group + 1) * count, :]
        turned = mixed[(groups + group) * count : (groups + group + 1) * count, :]
        mine = (lane < HD) == (group < half)
        heads.append(jnp.where(mine, straight, pltpu.roll(turned, HD, 1)).astype(BF16))
    heads = jnp.concatenate(heads, axis=1)
    for part, move in enumerate(parts):
        move.wait()
        here = slice(part * chunk, (part + 1) * chunk)
        out_ref[:, here] = dot(heads, proj[here, :], NT)


def attend(lengths, queries, new_kv, cache_kv, out_proj):
    steps, rows, width = queries.shape
    span = cache_kv.shape[1]
    proj = out_proj.T
    model_width = proj.shape[0]
    count = steps * rows
    groups = width // LANES
    fresh = new_kv.reshape(count * 2, LANES)
    cache = cache_kv.reshape(rows, 2 * span, LANES)
    return pl.pallas_call(
        attention_kernel,
        out_shape=vmem((count, model_width), F32),
        in_specs=[pl.BlockSpec(memory_space=pltpu.HBM)] * 5,
        out_specs=pl.BlockSpec(memory_space=pltpu.VMEM),
        scratch_shapes=[
            pltpu.SMEM(lengths.shape, jnp.int32),
            pltpu.VMEM(queries.shape, BF16),
            pltpu.VMEM(fresh.shape, BF16),
            pltpu.VMEM(cache.shape, BF16),
            pltpu.VMEM(proj.shape, BF16),
            pltpu.VMEM((rows + 1, 2 * span, LANES), F32),
            pltpu.VMEM((2 * groups * count, LANES), F32),
            pltpu.VMEM((2 * groups * count, LANES), F32),
            pltpu.SemaphoreType.DMA((8,)),
        ],
        compiler_params=params(16),
        cost_estimate=pl.CostEstimate(flops=1000, bytes_accessed=1000, transcendentals=0),
        name="attention",
    )(afar(lengths), afar(queries), afar(fresh), afar(cache), afar(proj))


def norm_kernel(residual_ref, mine_ref, other_ref, routing_ref, router_ref, mixed_ref, packed_ref):
    steps, rows, width = residual_ref.shape
    for step in range(steps):
        mixed_ref[step * rows : (step + 1) * rows, :] = residual_ref[step].astype(F32)
    mixed = mixed_ref[...] + (mine_ref[...] + other_ref[...])
    mixed_ref[...] = mixed
    scale = lax.rsqrt(jnp.mean(mixed * mixed, axis=1, keepdims=True) + 1e-05)
    normed = (mixed * scale).astype(BF16)
    logits = dot(normed, router_ref[...], NT)
    routing = routing_ref[...]
    expert = iota(logits.shape, 1)
    chosen = expert == routing[:, 0:1]
    for slot in range(1, TOP):
        chosen = chosen | (expert == routing[:, slot : slot + 1])
    sigmoids = jnp.where(chosen, jax.nn.sigmoid(logits), 0.0)
    gates = sigmoids / jnp.sum(sigmoids, axis=1, keepdims=True)
    high = gates.astype(BF16)
    low = (gates - high.astype(F32)).astype(BF16)
    first = width // LANES * LANES
    offset = width - first
    target = iota((EXPERTS, LANES), 1) - iota((EXPERTS, LANES), 0)
    tail = dot(high, (target == offset).astype(BF16)) + dot(low, (target == offset + EXPERTS).astype(BF16))
    packed_ref[:, :width] = normed
    packed_ref[:, width : width + LANES - offset] = tail[:, offset:].astype(BF16)


def normalize(residual, mine, other, routing, router):
    steps, rows, width = residual.shape
    count = steps * rows
    padded = -(-(width + 2 * EXPERTS) // LANES) * LANES
    return pl.pallas_call(
        norm_kernel,
        out_shape=(vmem((count, width), F32), vmem((count, padded), BF16)),
        in_specs=whole(5),
        out_specs=whole(2),
        compiler_params=params(),
        cost_estimate=pl.CostEstimate(flops=20_000_000_000, bytes_accessed=40_000_000, transcendentals=0),
        name="normalize",
    )(held(residual), held(mine), held(other), held(routing), held(router.T))


def weights_kernel(step, rows_ref, mantissa_ref, exponent_ref, member_ref, *refs):
    out_refs, table_ref, (power, expander) = refs[:-3], refs[-3], refs[-2:]
    units, blocks = power.shape
    width = expander.shape[1]

    experts = member_ref.shape[0]
    lane = iota((experts, LANES), 1) - iota((experts, LANES), 0) - width % LANES
    table_ref[...] = dot(member_ref[...], ((lane == 0) | (lane == experts)).astype(BF16), TN).astype(BF16)

    expander[...] = (iota((blocks, width), 1) // BLOCK == iota((blocks, width), 0)).astype(BF16)
    for part, out_ref in enumerate(out_refs):
        exponent = exponent_ref[part * blocks : (part + 1) * blocks, 0, :]
        power[...] = jnp.exp2(exponent.astype(F32)).T.astype(BF16)
        for first in range(0, units, step):
            here = slice(first, first + step)
            scale = dot(power[here, :], expander[...])
            out_ref[here, :] = (mantissa_ref[part, here, :].astype(F32) * scale).astype(BF16)


def dequantize(rows, mantissa, exponent, member):
    parts, units, width = mantissa.shape
    blocks = exponent.shape[0] // parts
    *weights, table = pl.pallas_call(
        functools.partial(weights_kernel, unit_step(units)),
        out_shape=(vmem((units, width), BF16),) * parts + (vmem((units, LANES), BF16),),
        in_specs=whole(4),
        out_specs=whole(parts + 1),
        scratch_shapes=[
            pltpu.VMEM((units, blocks), BF16),
            pltpu.VMEM((blocks, width), BF16),
        ],
        compiler_params=params(14),
        cost_estimate=pl.CostEstimate(flops=1000, bytes_accessed=1000, transcendentals=0),
        name="weights",
    )(held(rows), held(mantissa), held(exponent), held(member))
    return weights, table


def experts_kernel(gate_ref, up_ref, down_ref, member_ref, *refs):
    arrived, (mine_ref, other_ref, rows) = refs[:-3], refs[-3:]
    units, width = gate_ref.shape
    place = 0
    for ref in arrived:
        rows[place : place + ref.shape[0], :] = ref[...]
        place += ref.shape[0]
    inputs = rows[:, :width]
    gates = rows[:, rows.shape[1] - LANES :]
    step = unit_step(units)
    hidden = []
    for first in range(0, units, step):
        here = slice(first, first + step)
        gate = dot(gate_ref[here, :], inputs, NT)
        up = dot(up_ref[here, :], inputs, NT)
        share = dot(member_ref[here, :], gates, NT)
        hidden.append((gate * jax.nn.sigmoid(gate) * up * share).astype(BF16))
    hidden = jnp.concatenate(hidden, axis=0).T
    half = mine_ref.shape[0]
    for first in range(0, width, 512):
        here = slice(first, min(first + 512, width))
        total = dot(hidden, down_ref[:, here])
        mine_ref[:, here] = total[:half, :]
        other_ref[:, here] = total[half:, :].astype(BF16)


def unit_step(units):
    for step in range(240, 15, -16):
        if units % step == 0:
            return step
    return units


def run_experts(weights, member, arrived):
    units, width = weights[0].shape
    count = sum(block.shape[0] for block in arrived)
    padded = arrived[0].shape[1]
    return pl.pallas_call(
        experts_kernel,
        out_shape=(vmem((count // 2, width), F32), vmem((count // 2, width), BF16)),
        in_specs=whole(4 + len(arrived)),
        out_specs=whole(2),
        scratch_shapes=[pltpu.VMEM((count, padded), BF16)],
        compiler_params=params(16),
        cost_estimate=pl.CostEstimate(flops=1000, bytes_accessed=1000, transcendentals=0),
        name="experts",
    )(*[held(kind) for kind in weights], held(member), *[held(block) for block in arrived])


def local(kernel, name, shapes, *values):
    return pl.pallas_call(
        kernel,
        out_shape=[vmem(*shape) for shape in shapes],
        in_specs=whole(len(values)),
        out_specs=whole(len(shapes)),
        compiler_params=params(),
        name=name,
    )(*[held(value) for value in values])


def join_kernel(mine_ref, other_ref, *out_refs):
    count = out_refs[0].shape[0]
    for turn, out_ref in enumerate(out_refs):
        here = slice(turn * count, (turn + 1) * count)
        out_ref[...] = (mine_ref[here, :] + other_ref[here, :].astype(F32)).astype(out_ref.dtype)


def join(mine, other, count, kept):
    rows, width = mine.shape
    shapes = [((count, width), F32 if turn < kept else BF16) for turn in range(rows // count)]
    return local(join_kernel, "join", shapes, mine, other)


def merge_kernel(mine_ref, other_ref, out_ref):
    out_ref[...] = (mine_ref[...] + other_ref[...].astype(F32)).astype(BF16)


def merge(mine, other):
    return local(merge_kernel, "merge", [(mine.shape, BF16)], mine, other)[0]


def last_kernel(mixed_ref, mine_ref, other_ref, out_ref):
    steps, rows, _ = out_ref.shape
    result = (mixed_ref[...] + (mine_ref[...] + other_ref[...])).astype(BF16)
    for step in range(steps):
        out_ref[step] = result[step * rows : (step + 1) * rows, :]


def last(mixed, mine, other, shape):
    return pl.pallas_call(
        last_kernel,
        out_shape=jax.ShapeDtypeStruct(shape, BF16),
        in_specs=whole(3),
        out_specs=pl.BlockSpec(memory_space=pltpu.VMEM),
        compiler_params=params(),
        name="last",
    )(held(mixed), held(mine), held(other))


def swap(value):
    return lax.ppermute(value, "tensor", [(0, 1), (1, 0)])


def partners(count):
    share = count // 8
    even = list(range(count - 2, count // 2 - 1, -2))
    even = (even[:share], even[share:])
    odd = [[k + 1 for k in core] for core in even]
    near = tuple([k for k in range(count // 2 - 1, -1, -1) if (k + 1) % 4 // 2 == core] for core in range(2))

    def turns(far):
        return [
            [(2 * place + core, 2 * (place ^ far[core][turn]) + core) for place in range(count) for core in range(2)]
            for turn in range(len(far[0]))
        ]

    return turns(even), turns(odd), turns(near)


def per_device(residual, queries, new_kv, cache_kv, lengths, routing, router, out_proj, mantissa, exponent, placement):
    places = lax.axis_size("expert")
    steps, rows, width = residual.shape
    count = steps * rows
    units = mantissa.shape[1]
    tile = lax.axis_index("expert") * (units // TILE_UNITS) + jnp.arange(units) // TILE_UNITS
    member = jnp.any(placement.reshape(EXPERTS, -1, 1) == tile, axis=1).astype(BF16)
    even, odd, close = partners(places)
    turns = even + odd + close
    beside = [(2 * spot + core, 2 * (spot ^ 1) + core) for spot in range(places) for core in range(2)]
    both = ("expert", "tensor")

    partial = attend(lengths, queries, new_kv, cache_kv, out_proj)
    mantissa = mantissa[0].transpose(1, 0, 2)
    exponent = exponent.transpose(2, 3, 0, 1).reshape(-1, 1, units)

    mixed, packed = normalize(residual, partial, swap(partial), routing.reshape(count, TOP), router)
    near = [lax.ppermute(packed, both, pairs) for pairs in turns]
    weights, member = dequantize(packed, mantissa, exponent, member)
    near, weights, member = lax.optimization_barrier((near[::-1], weights, member))
    near = near[::-1]
    far = [swap(block) for block in near]
    mine, other = run_experts(weights, member, near + far)
    sums = join(mine, swap(other), count, len(even))
    passed = [lax.ppermute(block, both, beside) for block in sums[len(even) : 2 * len(even)]]
    back = [
        lax.ppermute(block, both, [(to, back) for back, to in pairs])
        for block, pairs in zip(sums[2 * len(even) :], close)
    ]
    back = [
        lax.ppermute(merge(block, extra), both, [(to, back) for back, to in pairs])
        for block, extra, pairs in zip(sums, passed, even)
    ] + back
    total = sum(block.astype(F32) for block in back)
    return last(mixed, total, swap(total), residual.shape)


def solution(mesh):
    placed = (
        P(None, ("group", "expert"), None),
        P(None, ("group", "expert"), "tensor"),
        P(None, ("group", "expert"), None, "tensor"),
        P(("group", "expert"), None, None, "tensor"),
        P(("group", "expert")),
        P(None, ("group", "expert"), None),
        P(),
        P("tensor", None),
        P("tensor", "expert", None, None),
        P("tensor", "expert", None, None),
        P("group"),
    )
    return jax.shard_map(
        per_device,
        mesh=mesh,
        in_specs=placed,
        out_specs=P(None, ("group", "expert"), None),
        check_vma=False,
    )
```

```python
import functools

import jax
import jax.numpy as jnp
from jax import lax
from jax.experimental import pallas as pl
from jax.experimental.pallas import tpu as pltpu
from jax.sharding import PartitionSpec as P

HD = 64
EXPERTS = 8
TOP = 4
BLOCK = 32
TILE_UNITS = 6
LANES = 128
F32 = jnp.float32
BF16 = jnp.bfloat16

NT = (((1,), (1,)), ((), ()))
TN = (((0,), (0,)), ((), ()))


def dot(a, b, dims=(((1,), (0,)), ((), ()))):
    return lax.dot_general(a, b, dims, preferred_element_type=F32)


def iota(shape, dim):
    return lax.broadcasted_iota(jnp.int32, shape, dim)


def vmem(shape, dtype):
    return pltpu.VMEM(shape, dtype)


def held(value):
    return pltpu.with_memory_space_constraint(value, pltpu.VMEM)


def afar(value):
    return pltpu.with_memory_space_constraint(value, pltpu.HBM)


def whole(count):
    return [pl.BlockSpec(memory_space=pltpu.VMEM)] * count


def params(mebibytes=8):
    return pltpu.CompilerParams(vmem_limit_bytes=mebibytes << 20)


def attention_kernel(
    lengths_hbm,
    queries_hbm,
    fresh_hbm,
    cache_hbm,
    proj_hbm,
    out_ref,
    lengths,
    queries,
    fresh_rows,
    cache_rows,
    proj,
    spread,
    packed,
    mixed,
    sems,
):
    moves = [
        pltpu.make_async_copy(source, target, sems.at[place])
        for place, (source, target) in enumerate(
            (
                (queries_hbm, queries),
                (lengths_hbm, lengths),
                (fresh_hbm, fresh_rows),
                (cache_hbm, cache_rows),
            )
        )
    ]
    chunk = proj.shape[0] // 4
    parts = [
        pltpu.make_async_copy(proj_hbm.at[pl.ds(part * chunk, chunk)], proj.at[pl.ds(part * chunk, chunk)], sems.at[4 + part])
        for part in range(4)
    ]
    for move in moves + parts[:2]:
        move.start()
    steps, rows, _ = queries.shape
    count = steps * rows
    groups = queries.shape[2] // LANES
    half = groups // 2
    lane = iota((rows, LANES), 1)
    moves[0].wait()
    for step in range(steps):
        for group in range(groups):
            piece = queries[step, :, group * LANES : (group + 1) * LANES].astype(F32) * (HD**-0.5)
            mine = (lane < HD) == (group < half)
            first = group * count + step * rows
            packed[first : first + rows, :] = jnp.where(mine, piece, 0.0)
            first += groups * count
            packed[first : first + rows, :] = jnp.where(mine, pltpu.roll(piece, HD, 1), 0.0)
    for move in parts[2:2]:
        move.start()
    amount = 2 * groups * steps
    span = cache_rows.shape[1] // 2
    spot = iota((amount, span), 1)
    step_of = iota((amount, count), 0) % steps
    fresh_spot = iota((amount, count), 1)
    for move in moves[1:4]:
        move.wait()
    for move in parts[2:]:
        move.start()

    def apart(value, which):
        size = value.shape[0]
        here = spread.at[which, :size]
        here[...] = value.astype(F32)
        return tuple(
            spread[which, pl.ds(first, size // 2, stride=2), :].astype(BF16) for first in range(2)
        )

    fresh_keys, fresh_values = apart(fresh_rows[...], rows)
    todo = []
    for row in range(rows):
        now = packed[pl.ds(row, amount, stride=rows), :].astype(BF16)
        keys, values = apart(cache_rows[row], row)
        todo.append((row, values, dot(now, keys, NT), dot(now, fresh_keys, NT)))
    probs = []
    for row, values, scores, late in todo:
        scores = jnp.where(spot < lengths[row], scores, -1e30)
        seen = (fresh_spot % rows == row) & (fresh_spot // rows <= step_of)
        late = jnp.where(seen, late, -1e30)
        highest = jnp.maximum(
            jnp.max(scores, axis=1, keepdims=True), jnp.max(late, axis=1, keepdims=True)
        )
        scores = jnp.exp(scores - highest)
        late = jnp.exp(late - highest)
        total = jnp.sum(scores, axis=1, keepdims=True) + jnp.sum(late, axis=1, keepdims=True)
        total = 1.0 / total
        probs.append((row, values, (scores * total).astype(BF16), (late * total).astype(BF16)))
    for row, values, scores, late in probs:
        mixed[pl.ds(row, amount, stride=rows), :] = dot(scores, values) + dot(late, fresh_values)
    heads = []
    lane = iota((count, LANES), 1)
    for group in range(groups):
        straight = mixed[group * count : (group + 1) * count, :]
        turned = mixed[(groups + group) * count : (groups + group + 1) * count, :]
        mine = (lane < HD) == (group < half)
        heads.append(jnp.where(mine, straight, pltpu.roll(turned, HD, 1)).astype(BF16))
    heads = jnp.concatenate(heads, axis=1)
    for part, move in enumerate(parts):
        move.wait()
        here = slice(part * chunk, (part + 1) * chunk)
        out_ref[:, here] = dot(heads, proj[here, :], NT)


def attend(lengths, queries, new_kv, cache_kv, out_proj):
    steps, rows, width = queries.shape
    span = cache_kv.shape[1]
    proj = out_proj.T
    model_width = proj.shape[0]
    count = steps * rows
    groups = width // LANES
    fresh = new_kv.reshape(count * 2, LANES)
    cache = cache_kv.reshape(rows, 2 * span, LANES)
    return pl.pallas_call(
        attention_kernel,
        out_shape=vmem((count, model_width), F32),
        in_specs=[pl.BlockSpec(memory_space=pltpu.HBM)] * 5,
        out_specs=pl.BlockSpec(memory_space=pltpu.VMEM),
        scratch_shapes=[
            pltpu.SMEM(lengths.shape, jnp.int32),
            pltpu.VMEM(queries.shape, BF16),
            pltpu.VMEM(fresh.shape, BF16),
            pltpu.VMEM(cache.shape, BF16),
            pltpu.VMEM(proj.shape, BF16),
            pltpu.VMEM((rows + 1, 2 * span, LANES), F32),
            pltpu.VMEM((2 * groups * count, LANES), F32),
            pltpu.VMEM((2 * groups * count, LANES), F32),
            pltpu.SemaphoreType.DMA((8,)),
        ],
        compiler_params=params(16),
        cost_estimate=pl.CostEstimate(flops=1000, bytes_accessed=1000, transcendentals=0),
        name="attention",
    )(afar(lengths), afar(queries), afar(fresh), afar(cache), afar(proj))


def norm_kernel(residual_ref, mine_ref, other_ref, routing_ref, router_ref, mixed_ref, packed_ref):
    steps, rows, width = residual_ref.shape
    for step in range(steps):
        mixed_ref[step * rows : (step + 1) * rows, :] = residual_ref[step].astype(F32)
    mixed = mixed_ref[...] + (mine_ref[...] + other_ref[...])
    mixed_ref[...] = mixed
    scale = lax.rsqrt(jnp.mean(mixed * mixed, axis=1, keepdims=True) + 1e-05)
    normed = (mixed * scale).astype(BF16)
    logits = dot(normed, router_ref[...], NT)
    routing = routing_ref[...]
    expert = iota(logits.shape, 1)
    chosen = expert == routing[:, 0:1]
    for slot in range(1, TOP):
        chosen = chosen | (expert == routing[:, slot : slot + 1])
    sigmoids = jnp.where(chosen, jax.nn.sigmoid(logits), 0.0)
    gates = sigmoids / jnp.sum(sigmoids, axis=1, keepdims=True)
    high = gates.astype(BF16)
    low = (gates - high.astype(F32)).astype(BF16)
    first = width // LANES * LANES
    offset = width - first
    target = iota((EXPERTS, LANES), 1) - iota((EXPERTS, LANES), 0)
    tail = dot(high, (target == offset).astype(BF16)) + dot(low, (target == offset + EXPERTS).astype(BF16))
    packed_ref[:, :width] = normed
    packed_ref[:, width : width + LANES - offset] = tail[:, offset:].astype(BF16)


def normalize(residual, mine, other, routing, router):
    steps, rows, width = residual.shape
    count = steps * rows
    padded = -(-(width + 2 * EXPERTS) // LANES) * LANES
    return pl.pallas_call(
        norm_kernel,
        out_shape=(vmem((count, width), F32), vmem((count, padded), BF16)),
        in_specs=whole(5),
        out_specs=whole(2),
        compiler_params=params(),
        cost_estimate=pl.CostEstimate(flops=20_000_000_000, bytes_accessed=40_000_000, transcendentals=0),
        name="normalize",
    )(held(residual), held(mine), held(other), held(routing), held(router.T))


def weights_kernel(step, rows_ref, mantissa_ref, exponent_ref, member_ref, *refs):
    out_refs, table_ref, (power, expander) = refs[:-3], refs[-3], refs[-2:]
    units, blocks = power.shape
    width = expander.shape[1]

    experts = member_ref.shape[0]
    lane = iota((experts, LANES), 1) - iota((experts, LANES), 0) - width % LANES
    table_ref[...] = dot(member_ref[...], ((lane == 0) | (lane == experts)).astype(BF16), TN).astype(BF16)

    expander[...] = (iota((blocks, width), 1) // BLOCK == iota((blocks, width), 0)).astype(BF16)
    for part, out_ref in enumerate(out_refs):
        exponent = exponent_ref[part * blocks : (part + 1) * blocks, 0, :]
        power[...] = jnp.exp2(exponent.astype(F32)).T.astype(BF16)
        for first in range(0, units, step):
            here = slice(first, first + step)
            scale = dot(power[here, :], expander[...])
            out_ref[here, :] = (mantissa_ref[part, here, :].astype(F32) * scale).astype(BF16)


def dequantize(rows, mantissa, exponent, member):
    parts, units, width = mantissa.shape
    blocks = exponent.shape[0] // parts
    *weights, table = pl.pallas_call(
        functools.partial(weights_kernel, unit_step(units)),
        out_shape=(vmem((units, width), BF16),) * parts + (vmem((units, LANES), BF16),),
        in_specs=whole(4),
        out_specs=whole(parts + 1),
        scratch_shapes=[
            pltpu.VMEM((units, blocks), BF16),
            pltpu.VMEM((blocks, width), BF16),
        ],
        compiler_params=params(14),
        cost_estimate=pl.CostEstimate(flops=1000, bytes_accessed=1000, transcendentals=0),
        name="weights",
    )(held(rows), held(mantissa), held(exponent), held(member))
    return weights, table


def experts_kernel(gate_ref, up_ref, down_ref, member_ref, *refs):
    arrived, (mine_ref, other_ref, rows) = refs[:-3], refs[-3:]
    units, width = gate_ref.shape
    place = 0
    for ref in arrived:
        rows[place : place + ref.shape[0], :] = ref[...]
        place += ref.shape[0]
    inputs = rows[:, :width]
    gates = rows[:, rows.shape[1] - LANES :]
    step = unit_step(units)
    hidden = []
    for first in range(0, units, step):
        here = slice(first, first + step)
        gate = dot(gate_ref[here, :], inputs, NT)
        up = dot(up_ref[here, :], inputs, NT)
        share = dot(member_ref[here, :], gates, NT)
        hidden.append((gate * jax.nn.sigmoid(gate) * up * share).astype(BF16))
    hidden = jnp.concatenate(hidden, axis=0).T
    half = mine_ref.shape[0]
    for first in range(0, width, 512):
        here = slice(first, min(first + 512, width))
        total = dot(hidden, down_ref[:, here])
        mine_ref[:, here] = total[:half, :]
        other_ref[:, here] = total[half:, :].astype(BF16)


def unit_step(units):
    for step in range(240, 15, -16):
        if units % step == 0:
            return step
    return units


def run_experts(weights, member, arrived):
    units, width = weights[0].shape
    count = sum(block.shape[0] for block in arrived)
    padded = arrived[0].shape[1]
    return pl.pallas_call(
        experts_kernel,
        out_shape=(vmem((count // 2, width), F32), vmem((count // 2, width), BF16)),
        in_specs=whole(4 + len(arrived)),
        out_specs=whole(2),
        scratch_shapes=[pltpu.VMEM((count, padded), BF16)],
        compiler_params=params(16),
        cost_estimate=pl.CostEstimate(flops=1000, bytes_accessed=1000, transcendentals=0),
        name="experts",
    )(*[held(kind) for kind in weights], held(member), *[held(block) for block in arrived])


def local(kernel, name, shapes, *values):
    return pl.pallas_call(
        kernel,
        out_shape=[vmem(*shape) for shape in shapes],
        in_specs=whole(len(values)),
        out_specs=whole(len(shapes)),
        compiler_params=params(),
        name=name,
    )(*[held(value) for value in values])


def join_kernel(mine_ref, other_ref, *out_refs):
    count = out_refs[0].shape[0]
    for turn, out_ref in enumerate(out_refs):
        here = slice(turn * count, (turn + 1) * count)
        out_ref[...] = (mine_ref[here, :] + other_ref[here, :].astype(F32)).astype(out_ref.dtype)


def join(mine, other, count, kept):
    rows, width = mine.shape
    shapes = [((count, width), F32 if turn < kept else BF16) for turn in range(rows // count)]
    return local(join_kernel, "join", shapes, mine, other)


def merge_kernel(mine_ref, other_ref, out_ref):
    out_ref[...] = (mine_ref[...] + other_ref[...].astype(F32)).astype(BF16)


def merge(mine, other):
    return local(merge_kernel, "merge", [(mine.shape, BF16)], mine, other)[0]


def last_kernel(mixed_ref, mine_ref, other_ref, out_ref):
    steps, rows, _ = out_ref.shape
    result = (mixed_ref[...] + (mine_ref[...] + other_ref[...])).astype(BF16)
    for step in range(steps):
        out_ref[step] = result[step * rows : (step + 1) * rows, :]


def last(mixed, mine, other, shape):
    return pl.pallas_call(
        last_kernel,
        out_shape=jax.ShapeDtypeStruct(shape, BF16),
        in_specs=whole(3),
        out_specs=pl.BlockSpec(memory_space=pltpu.VMEM),
        compiler_params=params(),
        name="last",
    )(held(mixed), held(mine), held(other))


def swap(value):
    return lax.ppermute(value, "tensor", [(0, 1), (1, 0)])


def partners(count):
    share = count // 8
    even = list(range(count - 2, count // 2 - 1, -2))
    even = (even[:share], even[share:])
    odd = [[k + 1 for k in core] for core in even]
    near = tuple([k for k in range(count // 2 - 1, -1, -1) if (k + 1) % 4 // 2 == core] for core in range(2))

    def turns(far):
        return [
            [(2 * place + core, 2 * (place ^ far[core][turn]) + core) for place in range(count) for core in range(2)]
            for turn in range(len(far[0]))
        ]

    return turns(even), turns(odd), turns(near)


def per_device(residual, queries, new_kv, cache_kv, lengths, routing, router, out_proj, mantissa, exponent, placement):
    places = lax.axis_size("expert")
    steps, rows, width = residual.shape
    count = steps * rows
    units = mantissa.shape[1]
    tile = lax.axis_index("expert") * (units // TILE_UNITS) + jnp.arange(units) // TILE_UNITS
    member = jnp.any(placement.reshape(EXPERTS, -1, 1) == tile, axis=1).astype(BF16)
    even, odd, close = partners(places)
    turns = even + odd + close
    beside = [(2 * spot + core, 2 * (spot ^ 1) + core) for spot in range(places) for core in range(2)]
    both = ("expert", "tensor")

    partial = attend(lengths, queries, new_kv, cache_kv, out_proj)
    mantissa = mantissa[0].transpose(1, 0, 2)
    exponent = exponent.transpose(2, 3, 0, 1).reshape(-1, 1, units)

    mixed, packed = normalize(residual, partial, swap(partial), routing.reshape(count, TOP), router)
    near = [lax.ppermute(packed, both, pairs) for pairs in turns]
    weights, member = dequantize(packed, mantissa, exponent, member)
    order = list(range(len(turns)))[::-1]
    order = order[: len(close)] + order[len(close) + len(odd) :] + order[len(close) : len(close) + len(odd)]
    arrived, weights, member = lax.optimization_barrier(([near[turn] for turn in order], weights, member))
    near = [arrived[order.index(turn)] for turn in range(len(turns))]
    far = [swap(block) for block in near]
    mine, other = run_experts(weights, member, near + far)
    sums = join(mine, swap(other), count, len(even))
    passed = [lax.ppermute(block, both, beside) for block in sums[len(even) : 2 * len(even)]]
    back = [
        lax.ppermute(block, both, [(to, back) for back, to in pairs])
        for block, pairs in zip(sums[2 * len(even) :], close)
    ]
    back = [
        lax.ppermute(merge(block, extra), both, [(to, back) for back, to in pairs])
        for block, extra, pairs in zip(sums, passed, even)
    ] + back
    total = sum(block.astype(F32) for block in back)
    return last(mixed, total, swap(total), residual.shape)


def solution(mesh):
    placed = (
        P(None, ("group", "expert"), None),
        P(None, ("group", "expert"), "tensor"),
        P(None, ("group", "expert"), None, "tensor"),
        P(("group", "expert"), None, None, "tensor"),
        P(("group", "expert")),
        P(None, ("group", "expert"), None),
        P(),
        P("tensor", None),
        P("tensor", "expert", None, None),
        P("tensor", "expert", None, None),
        P("group"),
    )
    return jax.shard_map(
        per_device,
        mesh=mesh,
        in_specs=placed,
        out_specs=P(None, ("group", "expert"), None),
        check_vma=False,
    )
```
